128 devices in a mesh: dp: 32 (over x, y, z_lo), mp: 4 (over z_hi, core).
Axes of the slice: x: 4, y: 4, z: 4 (z_hi: 2, z_lo: 2; z = z_hi * 2 + z_lo), core: 2. Of those that a mesh axis runs over, the one named last changes fastest.
Arguments:
- activations: bfloat16 [16384, 8192], P('dp', 'mp'), may hold values from -6 to 6
- out_grads: bfloat16 [16384, 1024], P('dp'), may hold values from -0.06591797 to 0.06591797
- projector: bfloat16 [8192, 512], P('mp'), may hold values from -0.0625 to 0.0625
- weight: float32 [8192, 1024], P('mp'), may hold values from -0.00024 to 0.00024
- first_moment: float32 [512, 1024], P('dp', 'mp'), may hold values from -0.6 to 0.6
- second_moment: float32 [512, 1024], P('dp', 'mp'), may hold values from 0.0003 to 0.003
Outputs:
- new_weight: float32 [8192, 1024], P('mp')
- update: bfloat16 [8192, 1024], P('mp')
- first_new: float32 [512, 1024], P('dp', 'mp')
- second_new: float32 [512, 1024], P('dp', 'mp')
The draws below stay inside these ranges and needn't reach their ends.
All inputs are finite; a program needn't handle non-finite values.
Results may differ from the reference program's by a relative error of at most 0.008.
Values may be sent and summed in bfloat16 or wider, within the bound.
A program may use at most 128 MiB of HBM per device.

```python
import math
import jax
import jax.numpy as jnp
from jax import lax

D = 8192
RANK = 512
COLS = 1024
TOKENS = 16384


def level_of(own_key, shape, pieces, least, high):
    def one(position, parts):
        heights = jax.random.uniform(jax.random.fold_in(jax.random.fold_in(own_key, 6), position), (parts,), jnp.float32, least / len(pieces), high / len(pieces))
        return jnp.repeat(jnp.exp(heights), shape[position] // parts).reshape((-1,) + (1,) * (len(shape) - position - 1))

    level = one(*pieces[0])
    for cut in pieces[1:]:
        level = level * one(*cut)
    return level


def gaussian(stream_key, dims, scale, limit, cuts=(), dtype=jnp.bfloat16):
    values = jax.random.normal(stream_key, dims, jnp.float32) * scale
    if len(cuts) > 0:
        values = level_of(stream_key, dims, cuts, -0.22, 0.18) * values
    return jnp.clip(values, min=-limit, max=limit).astype(dtype)


def setup_inputs(seed: int = 0) -> dict:
    arg_keys = jax.random.split(jax.random.key(seed), 7)
    return {
        "activations": gaussian(arg_keys[0], (TOKENS, D), 1.0, 6.0, ((0, 32), (1, 4))),
        "out_grads": gaussian(arg_keys[1], (TOKENS, COLS), 0.011, 0.06591797, ((0, 32),)),
        "projector": gaussian(arg_keys[2], (D, RANK), D ** -0.5, 0.0625, ((0, 4),)),
        "weight": gaussian(arg_keys[3], (D, COLS), 0.00004, 0.00024, ((0, 4),), jnp.float32),
        "first_moment": gaussian(arg_keys[4], (RANK, COLS), 0.1, 0.6, ((0, 32), (1, 4)), jnp.float32),
        "second_moment": jnp.clip(jnp.exp(math.log(0.003) - 2.3025851 * jax.random.uniform(arg_keys[5], (RANK, COLS), jnp.float32) ** level_of(arg_keys[5], (RANK, COLS), ((0, 32), (1, 4)), -0.2, 0.2)), 0.0003, 0.003),
    }


first_decay = 0.9
second_decay = 0.999
first_bias = 1.0 - 0.9 ** 2
second_bias = 1.0 - 0.999 ** 2
epsilon = 1e-08
step_rate = 0.00025

def reference(activations, out_grads, projector, weight, first_moment, second_moment):
    basis = projector.astype(jnp.float32)
    projected = jnp.dot(activations.astype(jnp.float32), basis, precision=lax.Precision.HIGHEST)
    coefficients = jnp.dot(projected.T, out_grads.astype(jnp.float32), precision=lax.Precision.HIGHEST)
    first_new = first_decay * first_moment + (1.0 - first_decay) * coefficients
    second_new = second_decay * second_moment + (1.0 - second_decay) * coefficients * coefficients
    normalized = (first_new / first_bias / (jnp.sqrt(second_new / second_bias) + epsilon)).astype(jnp.bfloat16)
    expanded = jnp.dot(basis, normalized.astype(jnp.float32), precision=lax.Precision.HIGHEST)
    new_weight = weight - step_rate * expanded
    return (new_weight, expanded.astype(jnp.bfloat16), first_new, second_new)
```

```python
import functools

import jax
import jax.numpy as jnp
from jax import lax
from jax.experimental import pallas as pl
from jax.experimental.pallas import tpu as pltpu
from jax.sharding import PartitionSpec as P

first_decay = 0.9
second_decay = 0.999
first_bias = 1.0 - 0.9**2
second_bias = 1.0 - 0.999**2
epsilon = 1e-08
step_rate = 0.00025

MESH = pl.DeviceIdType.MESH
F32 = jnp.float32
BF16 = jnp.bfloat16
TOKEN_CHUNKS = 4


def reduce_kernel(
    acts,
    grads,
    proj,
    first_moment,
    second_moment,
    gathered,
    first_new_ref,
    second_new_ref,
    acts_v,
    proj_v,
    grads_v,
    mine,
    theirs,
    summed,
    parts,
    got1,
    sums1,
    got2,
    sums2,
    got3,
    load_sem,
    pair_send,
    pair_recv,
    rs_send,
    rs_recv,
    ag_send,
    ag_recv,
    fw_send,
    fw_recv,
):
    dp = lax.axis_index("dp")
    mp = lax.axis_index("mp")
    x, y, zl = dp // 8, (dp // 2) % 4, dp % 2
    zh, c = mp // 2, mp % 2
    z = zh * 2 + zl

    def at_x(d):
        return (((x + d) % 4) * 8 + y * 2 + zl, mp)

    def at_y(d):
        return (x * 8 + ((y + d) % 4) * 2 + zl, mp)

    def at_z(d):
        to = (z + d) % 4
        return (x * 8 + y * 2 + to % 2, (to // 2) * 2 + c)

    sibling = (dp, zh * 2 + 1 - c)

    tokens = acts.shape[0]
    chunk = tokens // TOKEN_CHUNKS
    load_proj = pltpu.make_async_copy(proj, proj_v, load_sem.at[0])
    load_proj.start()
    load_acts = []
    for t in range(TOKEN_CHUNKS):
        rows = pl.ds(t * chunk, chunk)
        copy = pltpu.make_async_copy(acts.at[rows], acts_v.at[rows], load_sem.at[1 + t])
        copy.start()
        load_acts.append(copy)
    load_grads = []
    for h in range(2):
        columns = pl.ds(pl.multiple_of(h * 512 + c * 256, 256), 256)
        copy = pltpu.make_async_copy(
            grads.at[:, columns], grads_v.at[:, pl.ds(h * 256, 256)], load_sem.at[1 + TOKEN_CHUNKS + h]
        )
        copy.start()
        load_grads.append(copy)

    barrier = pltpu.get_barrier_semaphore()
    for partner in [sibling] + [at(d) for at in (at_x, at_y, at_z) for d in (1, 2, 3)]:
        pl.semaphore_signal(barrier, inc=1, device_id=partner, device_id_type=MESH)

    def remote(src, dst, send, recv, device):
        return pltpu.make_async_remote_copy(
            src_ref=src, dst_ref=dst, send_sem=send, recv_sem=recv, device_id=device, device_id_type=MESH
        )

    load_proj.wait()
    pair = []
    for t in range(TOKEN_CHUNKS):
        rows = pl.ds(t * chunk, chunk)
        load_acts[t].wait()
        projected = jnp.dot(acts_v[rows, :], proj_v[...], preferred_element_type=F32)
        mine[rows, :] = projected.astype(BF16)
        summed[rows, :] = projected
        if t == 0:
            pl.semaphore_wait(barrier, 10)
        copy = remote(mine.at[rows], theirs.at[rows], pair_send.at[t], pair_recv.at[t], sibling)
        copy.start()
        pair.append(copy)
    for copy in load_grads:
        copy.wait()
    for t in range(TOKEN_CHUNKS):
        rows = pl.ds(t * chunk, chunk)
        pair[t].wait()
        mine[rows, :] = (summed[rows, :] + theirs[rows, :].astype(F32)).astype(BF16)

    started = []
    for b in range(4):
        block = lax.dot_general(
            mine[:, b * 128 : (b + 1) * 128],
            grads_v[...],
            (((0,), (0,)), ((), ())),
            preferred_element_type=F32,
        ).astype(BF16)
        for h in range(2):
            for half in range(2):
                first = h * 256 + half * 128
                parts[h, half, b] = block[:, first : first + 128].reshape(4, 32, 128)

    stage = []
    for d in (2, 1, 3):
        a = remote(
            parts.at[:, 0, (x + d) % 4], got1.at[0, d - 1], rs_send.at[0, 0, d - 1], rs_recv.at[0, 0, d - 1], at_x(d)
        )
        b = remote(
            parts.at[:, 1, :, (y + d) % 4], got1.at[1, d - 1], rs_send.at[0, 1, d - 1], rs_recv.at[0, 1, d - 1], at_y(d)
        )
        a.start()
        b.start()
        stage.append((a, b))
    started += [copy for both in stage for copy in both]
    for half in range(2):
        for both in stage:
            both[half].wait_recv()
        own = parts[:, 0, x] if half == 0 else parts[:, 1, :, y]
        total = own.astype(F32)
        for s in range(3):
            total += got1[half, s].astype(F32)
        sums1[half] = total.astype(BF16)
        again = []
        for d in (2, 1, 3):
            to, device = ((y + d) % 4, at_y(d)) if half == 0 else ((x + d) % 4, at_x(d))
            copy = remote(
                sums1.at[half, :, to],
                got2.at[half, d - 1],
                rs_send.at[1, half, d - 1],
                rs_recv.at[1, half, d - 1],
                device,
            )
            copy.start()
            again.append(copy)
        started += again
        if half == 0:
            second = [again]
        else:
            second.append(again)
    for half in range(2):
        for copy in second[half]:
            copy.wait_recv()
        own = sums1[half, :, y] if half == 0 else sums1[half, :, x]
        total = own.astype(F32)
        for s in range(3):
            total += got2[half, s].astype(F32)
        sums2[:, :, :, half * 128 : (half + 1) * 128] = total.reshape(2, 2, 16, 128)
    third = []
    for d in (2, 1, 3):
        to = (z + d) % 4
        copy = remote(
            sums2.at[to // 2, to % 2], got3.at[d - 1], rs_send.at[2, 0, d - 1], rs_recv.at[2, 0, d - 1], at_z(d)
        )
        copy.start()
        third.append(copy)
    started += third
    for copy in third:
        copy.wait_recv()
    coefficients = sums2[zh, zl] + got3[0] + got3[1] + got3[2]

    first_new = first_decay * first_moment[...] + (1.0 - first_decay) * coefficients
    second_new = second_decay * second_moment[...] + (1.0 - second_decay) * coefficients * coefficients
    first_new_ref[...] = first_new
    second_new_ref[...] = second_new
    normalized = first_new / first_bias / (jnp.sqrt(second_new / second_bias) + epsilon)
    normalized = normalized.astype(BF16)
    gathered[zh, c, 0, x, y, zl] = normalized[:, :128]
    gathered[zh, c, 1, x, y, zl] = normalized[:, 128:]

    def spread(src, send, recv, device):
        copy = remote(src, src, send, recv, device)
        copy.start()
        started.append(copy)
        return copy

    forwards = []

    def forward(src, n):
        forwards.append(spread(src, fw_send.at[n], fw_recv.at[n], sibling))

    ring = [
        (spread(gathered.at[zh, c, :, x, y, zl], ag_send.at[0, 0, d - 1], ag_recv.at[0, 0, d - 1], at_z(d)), d)
        for d in (2, 1, 3)
    ]
    for copy, d in ring:
        copy.wait_recv()
    ring_a, ring_b = [], []
    for d in (2, 1, 3):
        ring_a.append(
            (spread(gathered.at[:, c, 0, x, y], ag_send.at[1, 0, d - 1], ag_recv.at[1, 0, d - 1], at_y(d)), d)
        )
        ring_b.append(
            (spread(gathered.at[:, c, 1, x, y], ag_send.at[1, 1, d - 1], ag_recv.at[1, 1, d - 1], at_x(d)), d)
        )
    forward(gathered.at[:, c, :, x, y], 0)
    for copy, d in ring_a:
        copy.wait_recv()
    last_a, last_b = [], []
    for d in (2, 1, 3):
        last_a.append((spread(gathered.at[:, c, 0, x], ag_send.at[2, 0, d - 1], ag_recv.at[2, 0, d - 1], at_x(d)), d))
    for copy, d in ring_b:
        copy.wait_recv()
    for d in (2, 1, 3):
        last_b.append(
            (spread(gathered.at[:, c, 1, :, y], ag_send.at[2, 1, d - 1], ag_recv.at[2, 1, d - 1], at_y(d)), d)
        )
    for copy, d in ring_a:
        forward(gathered.at[:, c, 0, x, (y - d + 4) % 4], d)
    for copy, d in ring_b:
        forward(gathered.at[:, c, 1, (x - d + 4) % 4, y], 3 + d)
    for n in (1, 2, 0):
        copy, d = last_a[n]
        copy.wait_recv()
        forward(gathered.at[:, c, 0, (x - d + 4) % 4], 6 + d)
        copy, d = last_b[n]
        copy.wait_recv()
        forward(gathered.at[:, c, 1, :, (y - d + 4) % 4], 9 + d)
    for copy in forwards:
        copy.wait_recv()
    for copy in started:
        copy.wait_send()


def reduce_and_gather(acts, grads, proj, first_moment, second_moment):
    vmem = pl.BlockSpec(memory_space=pltpu.VMEM)
    hbm = pl.BlockSpec(memory_space=pl.ANY)
    dma = pltpu.SemaphoreType.DMA
    return pl.pallas_call(
        reduce_kernel,
        out_shape=(
            jax.ShapeDtypeStruct((2, 2, 2, 4, 4, 2, 16, 128), BF16),
            jax.ShapeDtypeStruct((16, 256), F32),
            jax.ShapeDtypeStruct((16, 256), F32),
        ),
        in_specs=[hbm, hbm, hbm, vmem, vmem],
        out_specs=(vmem, vmem, vmem),
        scratch_shapes=[
            pltpu.VMEM((512, 2048), BF16),
            pltpu.VMEM((2048, 512), BF16),
            pltpu.VMEM((512, 512), BF16),
            pltpu.VMEM((512, 512), BF16),
            pltpu.VMEM((512, 512), BF16),
            pltpu.VMEM((512, 512), F32),
            pltpu.VMEM((2, 2, 4, 4, 32, 128), BF16),
            pltpu.VMEM((2, 3, 2, 4, 32, 128), BF16),
            pltpu.VMEM((2, 2, 4, 32, 128), BF16),
            pltpu.VMEM((2, 3, 2, 32, 128), BF16),
            pltpu.VMEM((2, 2, 16, 256), F32),
            pltpu.VMEM((3, 16, 256), F32),
            dma((3 + TOKEN_CHUNKS,)),
            dma((TOKEN_CHUNKS,)),
            dma((TOKEN_CHUNKS,)),
            dma((3, 2, 3)),
            dma((3, 2, 3)),
            dma((3, 2, 3)),
            dma((3, 2, 3)),
            dma((13,)),
            dma((13,)),
        ],
        compiler_params=pltpu.CompilerParams(
            collective_id=0, has_side_effects=True, vmem_limit_bytes=24 * 1024 * 1024
        ),
    )(acts, grads, proj, first_moment, second_moment)


def expand_kernel(gathered, proj, weight, first_in, second_in, new_weight, update, first_out, second_out):
    @pl.when(pl.program_id(0) == 0)
    def _():
        first_out[...] = first_in[...]
        second_out[...] = second_in[...]

    rows = proj[...]
    for n in range(4):
        columns = slice(n * 256, (n + 1) * 256)
        block = jnp.concatenate([gathered[2 * n], gathered[2 * n + 1]], axis=1)
        expanded = jnp.dot(rows, block, preferred_element_type=F32)
        new_weight[:, columns] = weight[:, columns] - step_rate * expanded
        update[:, columns] = expanded.astype(BF16)


def expand(gathered, proj, weight, first_new, second_new):
    depth, rank = proj.shape
    tile = 256
    whole = lambda *shape: pl.BlockSpec(shape, lambda i: (0,) * len(shape))
    return pl.pallas_call(
        expand_kernel,
        grid=(depth // tile,),
        out_shape=(
            jax.ShapeDtypeStruct((depth, 1024), F32),
            jax.ShapeDtypeStruct((depth, 1024), BF16),
            jax.ShapeDtypeStruct((16, 256), F32),
            jax.ShapeDtypeStruct((16, 256), F32),
        ),
        in_specs=[
            whole(8, rank, 128),
            pl.BlockSpec((tile, rank), lambda i: (i, 0)),
            pl.BlockSpec((tile, 1024), lambda i: (i, 0)),
            whole(16, 256),
            whole(16, 256),
        ],
        out_specs=(
            pl.BlockSpec((tile, 1024), lambda i: (i, 0)),
            pl.BlockSpec((tile, 1024), lambda i: (i, 0)),
            whole(16, 256),
            whole(16, 256),
        ),
        compiler_params=pltpu.CompilerParams(vmem_limit_bytes=16 * 1024 * 1024),
    )(gathered, proj, weight, first_new, second_new)


def local(activations, out_grads, projector, weight, first_moment, second_moment):
    gathered, first_new, second_new = reduce_and_gather(
        activations, out_grads, projector, first_moment, second_moment
    )
    gathered = gathered.reshape(8, 512, 128)
    return tuple(expand(gathered, projector, weight, first_new, second_new))


def solution(mesh):
    in_specs = (
        P("dp", "mp"),
        P("dp", None),
        P("mp", None),
        P("mp", None),
        P("dp", "mp"),
        P("dp", "mp"),
    )
    out_specs = (P("mp", None), P("mp", None), P("dp", "mp"), P("dp", "mp"))
    return jax.shard_map(local, mesh=mesh, in_specs=in_specs, out_specs=out_specs, check_vma=False)
```

```python
import functools

import jax
import jax.numpy as jnp
from jax import lax
from jax.experimental import pallas as pl
from jax.experimental.pallas import tpu as pltpu
from jax.sharding import PartitionSpec as P

first_decay = 0.9
second_decay = 0.999
first_bias = 1.0 - 0.9**2
second_bias = 1.0 - 0.999**2
epsilon = 1e-08
step_rate = 0.00025

MESH = pl.DeviceIdType.MESH
F32 = jnp.float32
BF16 = jnp.bfloat16
TOKEN_CHUNKS = 4
ROW_TILE = 256


def reduce_kernel(
    acts,
    grads,
    proj,
    weight,
    first_moment,
    second_moment,
    gathered,
    proj_v,
    weight_v,
    first_new_ref,
    second_new_ref,
    acts_v,
    grads_v,
    first_v,
    second_v,
    mine,
    theirs,
    summed,
    parts,
    got1,
    sums1,
    got2,
    sums2,
    got3,
    load_sem,
    pair_send,
    pair_recv,
    rs_send,
    rs_recv,
    ag_send,
    ag_recv,
    fw_send,
    fw_recv,
):
    dp = lax.axis_index("dp")
    mp = lax.axis_index("mp")
    x, y, zl = dp // 8, (dp // 2) % 4, dp % 2
    zh, c = mp // 2, mp % 2
    z = zh * 2 + zl

    def at_x(d):
        return (((x + d) % 4) * 8 + y * 2 + zl, mp)

    def at_y(d):
        return (x * 8 + ((y + d) % 4) * 2 + zl, mp)

    def at_z(d):
        to = (z + d) % 4
        return (x * 8 + y * 2 + to % 2, (to // 2) * 2 + c)

    sibling = (dp, zh * 2 + 1 - c)

    tokens = acts.shape[0]
    chunk = tokens // TOKEN_CHUNKS
    load_proj = pltpu.make_async_copy(proj, proj_v, load_sem.at[0])
    load_proj.start()
    load_acts = []
    for t in range(TOKEN_CHUNKS):
        rows = pl.ds(t * chunk, chunk)
        copy = pltpu.make_async_copy(acts.at[rows], acts_v.at[rows], load_sem.at[1 + t])
        copy.start()
        load_acts.append(copy)
    load_grads = []
    for h in range(2):
        columns = pl.ds(pl.multiple_of(h * 512 + c * 256, 256), 256)
        copy = pltpu.make_async_copy(
            grads.at[:, columns], grads_v.at[:, pl.ds(h * 256, 256)], load_sem.at[1 + TOKEN_CHUNKS + h]
        )
        copy.start()
        load_grads.append(copy)
    load_late = []
    for n, (src, dst) in enumerate(((first_moment, first_v), (second_moment, second_v), (weight, weight_v))):
        copy = pltpu.make_async_copy(src, dst, load_sem.at[3 + TOKEN_CHUNKS + n])
        copy.start()
        load_late.append(copy)

    barrier = pltpu.get_barrier_semaphore()
    for partner in [sibling] + [at(d) for at in (at_x, at_y, at_z) for d in (1, 2, 3)]:
        pl.semaphore_signal(barrier, inc=1, device_id=partner, device_id_type=MESH)

    def remote(src, dst, send, recv, device):
        return pltpu.make_async_remote_copy(
            src_ref=src, dst_ref=dst, send_sem=send, recv_sem=recv, device_id=device, device_id_type=MESH
        )

    load_proj.wait()
    pair = []
    for t in range(TOKEN_CHUNKS):
        rows = pl.ds(t * chunk, chunk)
        load_acts[t].wait()
        projected = jnp.dot(acts_v[rows, :], proj_v[...], preferred_element_type=F32)
        mine[rows, :] = projected.astype(BF16)
        summed[rows, :] = projected
        if t == 0:
            pl.semaphore_wait(barrier, 10)
        copy = remote(mine.at[rows], theirs.at[rows], pair_send.at[t], pair_recv.at[t], sibling)
        copy.start()
        pair.append(copy)
    for copy in load_grads:
        copy.wait()
    for t in range(TOKEN_CHUNKS):
        rows = pl.ds(t * chunk, chunk)
        pair[t].wait()
        mine[rows, :] = (summed[rows, :] + theirs[rows, :].astype(F32)).astype(BF16)

    started = []
    for b in range(4):
        block = lax.dot_general(
            mine[:, b * 128 : (b + 1) * 128],
            grads_v[...],
            (((0,), (0,)), ((), ())),
            preferred_element_type=F32,
        ).astype(BF16)
        for h in range(2):
            for half in range(2):
                first = h * 256 + half * 128
                parts[h, half, b] = block[:, first : first + 128].reshape(4, 32, 128)

    stage = []
    for d in (2, 1, 3):
        a = remote(
            parts.at[:, 0, (x + d) % 4], got1.at[0, d - 1], rs_send.at[0, 0, d - 1], rs_recv.at[0, 0, d - 1], at_x(d)
        )
        b = remote(
            parts.at[:, 1, :, (y + d) % 4], got1.at[1, d - 1], rs_send.at[0, 1, d - 1], rs_recv.at[0, 1, d - 1], at_y(d)
        )
        a.start()
        b.start()
        stage.append((a, b))
    started += [copy for both in stage for copy in both]
    for half in range(2):
        for both in stage:
            both[half].wait_recv()
        own = parts[:, 0, x] if half == 0 else parts[:, 1, :, y]
        total = own.astype(F32)
        for s in range(3):
            total += got1[half, s].astype(F32)
        sums1[half] = total.astype(BF16)
        again = []
        for d in (2, 1, 3):
            to, device = ((y + d) % 4, at_y(d)) if half == 0 else ((x + d) % 4, at_x(d))
            copy = remote(
                sums1.at[half, :, to],
                got2.at[half, d - 1],
                rs_send.at[1, half, d - 1],
                rs_recv.at[1, half, d - 1],
                device,
            )
            copy.start()
            again.append(copy)
        started += again
        if half == 0:
            second = [again]
        else:
            second.append(again)
    for half in range(2):
        for copy in second[half]:
            copy.wait_recv()
        own = sums1[half, :, y] if half == 0 else sums1[half, :, x]
        total = own.astype(F32)
        for s in range(3):
            total += got2[half, s].astype(F32)
        sums2[:, :, :, half * 128 : (half + 1) * 128] = total.reshape(2, 2, 16, 128)
    third = []
    for d in (2, 1, 3):
        to = (z + d) % 4
        copy = remote(
            sums2.at[to // 2, to % 2], got3.at[d - 1], rs_send.at[2, 0, d - 1], rs_recv.at[2, 0, d - 1], at_z(d)
        )
        copy.start()
        third.append(copy)
    started += third
    for copy in third:
        copy.wait_recv()
    coefficients = sums2[zh, zl] + got3[0] + got3[1] + got3[2]

    load_late[0].wait()
    load_late[1].wait()
    first_new = first_decay * first_v[...] + (1.0 - first_decay) * coefficients
    second_new = second_decay * second_v[...] + (1.0 - second_decay) * coefficients * coefficients
    first_new_ref[...] = first_new
    second_new_ref[...] = second_new
    normalized = first_new / first_bias / (jnp.sqrt(second_new / second_bias) + epsilon)
    normalized = normalized.astype(BF16)
    gathered[zh, c, 0, x, y, zl] = normalized[:, :128]
    gathered[zh, c, 1, x, y, zl] = normalized[:, 128:]

    def spread(src, send, recv, device):
        copy = remote(src, src, send, recv, device)
        copy.start()
        started.append(copy)
        return copy

    forwards = []

    def forward(src, n):
        forwards.append(spread(src, fw_send.at[n], fw_recv.at[n], sibling))

    ring = [
        (spread(gathered.at[zh, c, :, x, y, zl], ag_send.at[0, 0, d - 1], ag_recv.at[0, 0, d - 1], at_z(d)), d)
        for d in (2, 1, 3)
    ]
    for copy, d in ring:
        copy.wait_recv()
    ring_a, ring_b = [], []
    for d in (2, 1, 3):
        ring_a.append(
            (spread(gathered.at[:, c, 0, x, y], ag_send.at[1, 0, d - 1], ag_recv.at[1, 0, d - 1], at_y(d)), d)
        )
        ring_b.append(
            (spread(gathered.at[:, c, 1, x, y], ag_send.at[1, 1, d - 1], ag_recv.at[1, 1, d - 1], at_x(d)), d)
        )
    forward(gathered.at[:, c, :, x, y], 0)
    for copy, d in ring_a:
        copy.wait_recv()
    last_a, last_b = [], []
    for d in (2, 1, 3):
        last_a.append((spread(gathered.at[:, c, 0, x], ag_send.at[2, 0, d - 1], ag_recv.at[2, 0, d - 1], at_x(d)), d))
    for copy, d in ring_b:
        copy.wait_recv()
    for d in (2, 1, 3):
        last_b.append(
            (spread(gathered.at[:, c, 1, :, y], ag_send.at[2, 1, d - 1], ag_recv.at[2, 1, d - 1], at_y(d)), d)
        )
    for copy, d in ring_a:
        forward(gathered.at[:, c, 0, x, (y - d + 4) % 4], d)
    for copy, d in ring_b:
        forward(gathered.at[:, c, 1, (x - d + 4) % 4, y], 3 + d)
    for n in (1, 2, 0):
        copy, d = last_a[n]
        copy.wait_recv()
        forward(gathered.at[:, c, 0, (x - d + 4) % 4], 6 + d)
        copy, d = last_b[n]
        copy.wait_recv()
        forward(gathered.at[:, c, 1, :, (y - d + 4) % 4], 9 + d)
    for copy in forwards:
        copy.wait_recv()
    for copy in started:
        copy.wait_send()
    load_late[2].wait()


def reduce_and_gather(*operands):
    proj, weight = operands[2], operands[3]
    vmem = pl.BlockSpec(memory_space=pltpu.VMEM)
    hbm = pl.BlockSpec(memory_space=pltpu.HBM)
    dma = pltpu.SemaphoreType.DMA
    return pl.pallas_call(
        reduce_kernel,
        out_shape=(
            pltpu.VMEM((2, 2, 2, 4, 4, 2, 16, 128), BF16),
            pltpu.VMEM(proj.shape, BF16),
            pltpu.VMEM(weight.shape, F32),
            pltpu.VMEM((16, 256), F32),
            pltpu.VMEM((16, 256), F32),
        ),
        in_specs=[hbm] * 6,
        out_specs=(vmem,) * 5,
        scratch_shapes=[
            pltpu.VMEM((512, 2048), BF16),
            pltpu.VMEM((512, 512), BF16),
            pltpu.VMEM((16, 256), F32),
            pltpu.VMEM((16, 256), F32),
            pltpu.VMEM((512, 512), BF16),
            pltpu.VMEM((512, 512), BF16),
            pltpu.VMEM((512, 512), F32),
            pltpu.VMEM((2, 2, 4, 4, 32, 128), BF16),
            pltpu.VMEM((2, 3, 2, 4, 32, 128), BF16),
            pltpu.VMEM((2, 2, 4, 32, 128), BF16),
            pltpu.VMEM((2, 3, 2, 32, 128), BF16),
            pltpu.VMEM((2, 2, 16, 256), F32),
            pltpu.VMEM((3, 16, 256), F32),
            dma((6 + TOKEN_CHUNKS,)),
            dma((TOKEN_CHUNKS,)),
            dma((TOKEN_CHUNKS,)),
            dma((3, 2, 3)),
            dma((3, 2, 3)),
            dma((3, 2, 3)),
            dma((3, 2, 3)),
            dma((13,)),
            dma((13,)),
        ],
        compiler_params=pltpu.CompilerParams(
            collective_id=0, has_side_effects=True, vmem_limit_bytes=24 * 1024 * 1024
        ),
    )(*(pltpu.with_memory_space_constraint(a, pltpu.HBM) for a in operands))


def expand_kernel(
    gathered,
    proj,
    weight,
    first_in,
    second_in,
    new_weight,
    update,
    first_out,
    second_out,
    new_v,
    update_v,
    sems,
    state_sems,
):
    states = [
        pltpu.make_async_copy(first_in, first_out, state_sems.at[0]),
        pltpu.make_async_copy(second_in, second_out, state_sems.at[1]),
    ]
    for copy in states:
        copy.start()

    def stores(i):
        rows = pl.ds(i * ROW_TILE, ROW_TILE)
        return (
            pltpu.make_async_copy(new_v.at[rows], new_weight.at[rows], sems.at[0, i]),
            pltpu.make_async_copy(update_v.at[rows], update.at[rows], sems.at[1, i]),
        )

    tiles = weight.shape[0] // ROW_TILE
    for i in range(tiles):
        rows = pl.ds(i * ROW_TILE, ROW_TILE)
        left = proj[rows, :]
        for n in range(4):
            columns = slice(n * 256, (n + 1) * 256)
            block = jnp.concatenate([gathered[2 * n], gathered[2 * n + 1]], axis=1)
            expanded = jnp.dot(left, block, preferred_element_type=F32)
            new_v[rows, columns] = weight[rows, columns] - step_rate * expanded
            update_v[rows, columns] = expanded.astype(BF16)
        for copy in stores(i):
            copy.start()
    for i in range(tiles):
        for copy in stores(i):
            copy.wait()
    for copy in states:
        copy.wait()


def expand(gathered, proj, weight, first_new, second_new):
    depth, rank = proj.shape
    vmem = pl.BlockSpec(memory_space=pltpu.VMEM)
    hbm = pl.BlockSpec(memory_space=pltpu.HBM)
    return pl.pallas_call(
        expand_kernel,
        out_shape=(
            jax.ShapeDtypeStruct((depth, 1024), F32),
            jax.ShapeDtypeStruct((depth, 1024), BF16),
            jax.ShapeDtypeStruct((16, 256), F32),
            jax.ShapeDtypeStruct((16, 256), F32),
        ),
        in_specs=[vmem] * 5,
        out_specs=(hbm,) * 4,
        scratch_shapes=[
            pltpu.VMEM((depth, 1024), F32),
            pltpu.VMEM((depth, 1024), BF16),
            pltpu.SemaphoreType.DMA((2, depth // ROW_TILE)),
            pltpu.SemaphoreType.DMA((2,)),
        ],
        compiler_params=pltpu.CompilerParams(vmem_limit_bytes=20 * 1024 * 1024),
    )(gathered, proj, weight, first_new, second_new)


def local(activations, out_grads, projector, weight, first_moment, second_moment):
    gathered, projector, weight, first_new, second_new = reduce_and_gather(
        activations, out_grads, projector, weight, first_moment, second_moment
    )
    gathered = gathered.reshape(8, 512, 128)
    return tuple(expand(gathered, projector, weight, first_new, second_new))


def solution(mesh):
    in_specs = (
        P("dp", "mp"),
        P("dp", None),
        P("mp", None),
        P("mp", None),
        P("dp", "mp"),
        P("dp", "mp"),
    )
    out_specs = (P("mp", None), P("mp", None), P("dp", "mp"), P("dp", "mp"))
    return jax.shard_map(local, mesh=mesh, in_specs=in_specs, out_specs=out_specs, check_vma=False)
```

```python
import functools

import jax
import jax.numpy as jnp
from jax import lax
from jax.experimental import pallas as pl
from jax.experimental.pallas import tpu as pltpu
from jax.sharding import PartitionSpec as P

first_decay = 0.9
second_decay = 0.999
first_bias = 1.0 - 0.9**2
second_bias = 1.0 - 0.999**2
epsilon = 1e-08
step_rate = 0.00025

MESH = pl.DeviceIdType.MESH
F32 = jnp.float32
BF16 = jnp.bfloat16
TOKEN_CHUNKS = 4
ROW_TILE = 256


def place(half, v):
    return ((v + v // 2) % 2, v // 2) if half == 0 else (v // 2, v % 2)


MASKS = (7, 6, 5, 3, 4, 2, 1)


def bits(m):
    return m // 4, m // 2 % 2, m % 2


def reduce_kernel(
    acts,
    grads,
    proj,
    weight,
    first_moment,
    second_moment,
    gathered,
    proj_v,
    weight_v,
    first_new_ref,
    second_new_ref,
    acts_v,
    grads_v,
    first_v,
    second_v,
    mine,
    theirs,
    both,
    summed,
    parts,
    got1,
    sums,
    got2,
    load_sem,
    pair_send,
    pair_recv,
    rs_send,
    rs_recv,
    ag_send,
    ag_recv,
    fw_send,
    fw_recv,
):
    dp = lax.axis_index("dp")
    mp = lax.axis_index("mp")
    zh, c = mp // 2, mp % 2
    chip = (dp // 8, (dp // 2) % 4, zh * 2 + dp % 2)
    sibling = (dp, zh * 2 + 1 - c)

    def partner(wrap, m):
        x, y, z = ((3 - v if wrap else v + 1 - 2 * (v % 2)) if bit else v for v, bit in zip(chip, bits(m)))
        return (x * 8 + y * 2 + z % 2, (z // 2) * 2 + c)

    def flip(at, m):
        return tuple(1 - v if bit else v for v, bit in zip(at, bits(m)))

    sets, members = [], []
    for half in range(2):
        places = [place(half, v) for v in chip]
        sets.append(tuple(p[0] for p in places))
        members.append(tuple(p[1] for p in places))

    tokens = acts.shape[0]
    chunk = tokens // TOKEN_CHUNKS
    load_proj = pltpu.make_async_copy(proj, proj_v, load_sem.at[0])
    load_proj.start()
    load_acts = []
    for t in range(TOKEN_CHUNKS):
        rows = pl.ds(t * chunk, chunk)
        copy = pltpu.make_async_copy(acts.at[rows], acts_v.at[rows], load_sem.at[1 + t])
        copy.start()
        load_acts.append(copy)
    load_grads = []
    for h in range(2):
        columns = pl.ds(pl.multiple_of(h * 512 + c * 256, 256), 256)
        copy = pltpu.make_async_copy(
            grads.at[:, columns], grads_v.at[:, pl.ds(h * 256, 256)], load_sem.at[1 + TOKEN_CHUNKS + h]
        )
        copy.start()
        load_grads.append(copy)
    load_late = [
        pltpu.make_async_copy(src, dst, load_sem.at[3 + TOKEN_CHUNKS + n])
        for n, (src, dst) in enumerate(((first_moment, first_v), (second_moment, second_v), (weight, weight_v)))
    ]
    load_late[0].start()
    load_late[1].start()

    barrier = pltpu.get_barrier_semaphore()
    for device in [sibling] + [partner(wrap, m) for wrap in (False, True) for m in MASKS]:
        pl.semaphore_signal(barrier, inc=1, device_id=device, device_id_type=MESH)

    started = []

    def send(src, dst, send_sem, recv_sem, device):
        copy = pltpu.make_async_remote_copy(
            src_ref=src, dst_ref=dst, send_sem=send_sem, recv_sem=recv_sem, device_id=device, device_id_type=MESH
        )
        copy.start()
        started.append(copy)
        return copy

    load_proj.wait()
    pair = []
    for t in range(TOKEN_CHUNKS):
        rows = pl.ds(t * chunk, chunk)
        load_acts[t].wait()
        projected = jnp.dot(acts_v[rows, :], proj_v[...], preferred_element_type=F32)
        mine[rows, :] = projected.astype(BF16)
        summed[rows, :] = projected
        if t == 0:
            pl.semaphore_wait(barrier, 15)
        pair.append(send(mine.at[rows], theirs.at[rows], pair_send.at[t], pair_recv.at[t], sibling))
    for copy in load_grads:
        copy.wait()
    load_late[2].start()
    for t in range(TOKEN_CHUNKS):
        rows = pl.ds(t * chunk, chunk)
        pair[t].wait_recv()
        both[rows, :] = (summed[rows, :] + theirs[rows, :].astype(F32)).astype(BF16)

    for x in range(4):
        block = lax.dot_general(
            both[:, x * 128 : (x + 1) * 128],
            grads_v[...],
            (((0,), (0,)), ((), ())),
            preferred_element_type=F32,
        ).astype(BF16)
        for y in range(4):
            for z in range(4):
                row = y * 32 + z % 2 * 16
                for half in range(2):
                    column = z // 2 * 256 + half * 128
                    at = [place(half, v) for v in (x, y, z)]
                    index = tuple(p[0] for p in at) + tuple(p[1] for p in at)
                    parts[(half, *index)] = block[row : row + 16, column : column + 128]

    stage1 = ([], [])
    for n, m in enumerate(MASKS):
        for half in range(2):
            to = flip(sets[half], m)
            stage1[half].append(
                send(
                    parts.at[(half, *to)],
                    got1.at[half, n],
                    rs_send.at[0, half, n],
                    rs_recv.at[0, half, n],
                    partner(half == 1, m),
                )
            )
    stage2 = ([], [])
    for half in range(2):
        for copy in stage1[half]:
            copy.wait_recv()
        total = parts[(half, *sets[half])].astype(F32)
        for n in range(7):
            total += got1[half, n].astype(F32)
        sums[half] = total.astype(BF16)
        for n, m in enumerate(MASKS):
            to = flip(members[half], m)
            stage2[half].append(
                send(
                    sums.at[(half, *to)],
                    got2.at[half, n],
                    rs_send.at[1, half, n],
                    rs_recv.at[1, half, n],
                    partner(half == 0, m),
                )
            )
    load_late[0].wait()
    load_late[1].wait()
    gather1 = ([], [])
    for half in range(2):
        for copy in stage2[half]:
            copy.wait_recv()
        coefficients = sums[(half, *members[half])].astype(F32)
        for n in range(7):
            coefficients += got2[half, n].astype(F32)

        columns = slice(half * 128, (half + 1) * 128)
        first_new = first_decay * first_v[:, columns] + (1.0 - first_decay) * coefficients
        second_new = second_decay * second_v[:, columns] + (1.0 - second_decay) * coefficients * coefficients
        first_new_ref[:, columns] = first_new
        second_new_ref[:, columns] = second_new
        normalized = first_new / first_bias / (jnp.sqrt(second_new / second_bias) + epsilon)
        own = (c, half, *sets[half], *members[half])
        gathered[own] = normalized.astype(BF16)

        for n, m in enumerate(MASKS):
            block = gathered.at[own]
            gather1[half].append(
                send(block, block, ag_send.at[0, half, n], ag_recv.at[0, half, n], partner(half == 0, m))
            )
    gather2 = ([], [])
    forwards = []

    def forward(half, at, n):
        block = gathered.at[(c, half, *at)]
        forwards.append(send(block, block, fw_send.at[half, n], fw_recv.at[half, n], sibling))

    for half in range(2):
        for copy in gather1[half]:
            copy.wait_recv()
        block = gathered.at[(c, half, *sets[half])]
        for n, m in enumerate(MASKS):
            gather2[half].append(
                send(block, block, ag_send.at[1, half, n], ag_recv.at[1, half, n], partner(half == 1, m))
            )
        forward(half, sets[half], 7)
    for n in reversed(range(7)):
        for half in range(2):
            gather2[half][n].wait_recv()
            forward(half, flip(sets[half], MASKS[n]), n)
    for copy in forwards:
        copy.wait_recv()
    for copy in started:
        copy.wait_send()
    load_late[2].wait()


def reduce_and_gather(*operands):
    proj, weight = operands[2], operands[3]
    vmem = pl.BlockSpec(memory_space=pltpu.VMEM)
    hbm = pl.BlockSpec(memory_space=pltpu.HBM)
    dma = pltpu.SemaphoreType.DMA
    return pl.pallas_call(
        reduce_kernel,
        out_shape=(
            pltpu.VMEM((2, 2, 2, 2, 2, 2, 2, 2, 16, 128), BF16),
            pltpu.VMEM(proj.shape, BF16),
            pltpu.VMEM(weight.shape, F32),
            pltpu.VMEM((16, 256), F32),
            pltpu.VMEM((16, 256), F32),
        ),
        in_specs=[hbm] * 6,
        out_specs=(vmem,) * 5,
        scratch_shapes=[
            pltpu.VMEM((512, 2048), BF16),
            pltpu.VMEM((512, 512), BF16),
            pltpu.VMEM((16, 256), F32),
            pltpu.VMEM((16, 256), F32),
            pltpu.VMEM((512, 512), BF16),
            pltpu.VMEM((512, 512), BF16),
            pltpu.VMEM((512, 512), BF16),
            pltpu.VMEM((512, 512), F32),
            pltpu.VMEM((2, 2, 2, 2, 2, 2, 2, 16, 128), BF16),
            pltpu.VMEM((2, 7, 2, 2, 2, 16, 128), BF16),
            pltpu.VMEM((2, 2, 2, 2, 16, 128), BF16),
            pltpu.VMEM((2, 7, 16, 128), BF16),
            dma((6 + TOKEN_CHUNKS,)),
            dma((TOKEN_CHUNKS,)),
            dma((TOKEN_CHUNKS,)),
            dma((2, 2, 7)),
            dma((2, 2, 7)),
            dma((2, 2, 7)),
            dma((2, 2, 7)),
            dma((2, 8)),
            dma((2, 8)),
        ],
        compiler_params=pltpu.CompilerParams(
            collective_id=0, has_side_effects=True, vmem_limit_bytes=24 * 1024 * 1024
        ),
    )(*(pltpu.with_memory_space_constraint(a, pltpu.HBM) for a in operands))


def expand_kernel(
    gathered,
    proj,
    weight,
    first_in,
    second_in,
    new_weight,
    update,
    first_out,
    second_out,
    ordered,
    new_v,
    update_v,
    sems,
    state_sems,
):
    states = [
        pltpu.make_async_copy(first_in, first_out, state_sems.at[0]),
        pltpu.make_async_copy(second_in, second_out, state_sems.at[1]),
    ]
    for copy in states:
        copy.start()

    def stores(i):
        rows = pl.ds(i * ROW_TILE, ROW_TILE)
        return (
            pltpu.make_async_copy(new_v.at[rows], new_weight.at[rows], sems.at[0, i]),
            pltpu.make_async_copy(update_v.at[rows], update.at[rows], sems.at[1, i]),
        )

    for zh in range(2):
        for c in range(2):
            for half in range(2):
                column = zh * 512 + c * 256 + half * 128
                for x in range(4):
                    for y in range(4):
                        for zl in range(2):
                            at = [place(half, v) for v in (x, y, zh * 2 + zl)]
                            index = tuple(p[0] for p in at) + tuple(p[1] for p in at)
                            row = x * 128 + y * 32 + zl * 16
                            ordered[row : row + 16, column : column + 128] = gathered[(c, half, *index)]

    tiles = weight.shape[0] // ROW_TILE
    for i in range(tiles):
        rows = pl.ds(i * ROW_TILE, ROW_TILE)
        left = proj[rows, :]
        for n in range(4):
            columns = slice(n * 256, (n + 1) * 256)
            expanded = jnp.dot(left, ordered[:, columns], preferred_element_type=F32)
            new_v[rows, columns] = weight[rows, columns] - step_rate * expanded
            update_v[rows, columns] = expanded.astype(BF16)
        for copy in stores(i):
            copy.start()
    for i in range(tiles):
        for copy in stores(i):
            copy.wait()
    for copy in states:
        copy.wait()


def expand(gathered, proj, weight, first_new, second_new):
    depth, rank = proj.shape
    vmem = pl.BlockSpec(memory_space=pltpu.VMEM)
    hbm = pl.BlockSpec(memory_space=pltpu.HBM)
    return pl.pallas_call(
        expand_kernel,
        out_shape=(
            jax.ShapeDtypeStruct((depth, 1024), F32),
            jax.ShapeDtypeStruct((depth, 1024), BF16),
            jax.ShapeDtypeStruct((16, 256), F32),
            jax.ShapeDtypeStruct((16, 256), F32),
        ),
        in_specs=[vmem] * 5,
        out_specs=(hbm,) * 4,
        scratch_shapes=[
            pltpu.VMEM((rank, 1024), BF16),
            pltpu.VMEM((depth, 1024), F32),
            pltpu.VMEM((depth, 1024), BF16),
            pltpu.SemaphoreType.DMA((2, depth // ROW_TILE)),
            pltpu.SemaphoreType.DMA((2,)),
        ],
        compiler_params=pltpu.CompilerParams(vmem_limit_bytes=20 * 1024 * 1024),
    )(gathered, proj, weight, first_new, second_new)


def local(activations, out_grads, projector, weight, first_moment, second_moment):
    gathered, projector, weight, first_new, second_new = reduce_and_gather(
        activations, out_grads, projector, weight, first_moment, second_moment
    )
    return tuple(expand(gathered, projector, weight, first_new, second_new))


def solution(mesh):
    in_specs = (
        P("dp", "mp"),
        P("dp", None),
        P("mp", None),
        P("mp", None),
        P("dp", "mp"),
        P("dp", "mp"),
    )
    out_specs = (P("mp", None), P("mp", None), P("dp", "mp"), P("dp", "mp"))
    return jax.shard_map(local, mesh=mesh, in_specs=in_specs, out_specs=out_specs, check_vma=False)
```

```python
import functools

import jax
import jax.numpy as jnp
from jax import lax
from jax.experimental import pallas as pl
from jax.experimental.pallas import tpu as pltpu
from jax.sharding import PartitionSpec as P

first_decay = 0.9
second_decay = 0.999
first_bias = 1.0 - 0.9**2
second_bias = 1.0 - 0.999**2
epsilon = 1e-08
step_rate = 0.00025

MESH = pl.DeviceIdType.MESH
F32 = jnp.float32
BF16 = jnp.bfloat16
TOKEN_CHUNKS = 4
ROW_TILE = 256


def place(half, v):
    return ((v + v // 2) % 2, v // 2) if half == 0 else (v // 2, v % 2)


MASKS = (7, 6, 5, 3, 4, 2, 1)


def bits(m):
    return m // 4, m // 2 % 2, m % 2


def reduce_kernel(
    acts,
    grads,
    proj,
    weight,
    first_moment,
    second_moment,
    gathered,
    proj_v,
    weight_v,
    first_new_ref,
    second_new_ref,
    acts_v,
    grads_v,
    mine,
    theirs,
    both,
    summed,
    parts,
    got1,
    sums,
    moments,
    states,
    load_sem,
    pair_send,
    pair_recv,
    send_sem,
    recv_sem,
    fw_send,
    fw_recv,
):
    dp = lax.axis_index("dp")
    mp = lax.axis_index("mp")
    zh, c = mp // 2, mp % 2
    chip = (dp // 8, (dp // 2) % 4, zh * 2 + dp % 2)
    sibling = (dp, zh * 2 + 1 - c)

    def partner(wrap, m):
        x, y, z = ((3 - v if wrap else v + 1 - 2 * (v % 2)) if bit else v for v, bit in zip(chip, bits(m)))
        return (x * 8 + y * 2 + z % 2, (z // 2) * 2 + c)

    def flip(at, m):
        return tuple(1 - v if bit else v for v, bit in zip(at, bits(m)))

    sets, members = [], []
    for half in range(2):
        places = [place(half, v) for v in chip]
        sets.append(tuple(p[0] for p in places))
        members.append(tuple(p[1] for p in places))

    tokens = acts.shape[0]
    chunk = tokens // TOKEN_CHUNKS
    load_proj = pltpu.make_async_copy(proj, proj_v, load_sem.at[0])
    load_proj.start()
    load_acts = []
    for t in range(TOKEN_CHUNKS):
        rows = pl.ds(t * chunk, chunk)
        copy = pltpu.make_async_copy(acts.at[rows], acts_v.at[rows], load_sem.at[1 + t])
        copy.start()
        load_acts.append(copy)
    load_grads = []
    for half in range(2):
        for h in range(2):
            columns = pl.ds(pl.multiple_of(h * 512 + c * 256 + half * 128, 128), 128)
            copy = pltpu.make_async_copy(
                grads.at[:, columns],
                grads_v.at[half, :, pl.ds(h * 128, 128)],
                load_sem.at[1 + TOKEN_CHUNKS + 2 * half + h],
            )
            copy.start()
            load_grads.append(copy)
    load_moments = []
    for half in range(2):
        columns = pl.ds(half * 128, 128)
        for n, moment in enumerate((first_moment, second_moment)):
            copy = pltpu.make_async_copy(
                moment.at[:, columns],
                moments.at[(half, *members[half], n)],
                load_sem.at[5 + TOKEN_CHUNKS + 2 * half + n],
            )
            copy.start()
            load_moments.append(copy)
    load_weight = pltpu.make_async_copy(weight, weight_v, load_sem.at[9 + TOKEN_CHUNKS])

    barrier = pltpu.get_barrier_semaphore()
    for device in [sibling] + [partner(wrap, m) for wrap in (False, True) for m in MASKS]:
        pl.semaphore_signal(barrier, inc=1, device_id=device, device_id_type=MESH)

    started = []

    def send(src, dst, sent, arrived, device):
        copy = pltpu.make_async_remote_copy(
            src_ref=src, dst_ref=dst, send_sem=sent, recv_sem=arrived, device_id=device, device_id_type=MESH
        )
        copy.start()
        started.append(copy)
        return copy

    def spread(stage, half, flips, source, target=None):
        copies = []
        for n, m in enumerate(MASKS):
            src = source(m)
            dst = src if target is None else target(n)
            device = partner((half == 1) == (flips == 1), m)
            copies.append(send(src, dst, send_sem.at[stage, half, n], recv_sem.at[stage, half, n], device))
        return copies

    load_proj.wait()
    pair = []
    for t in range(TOKEN_CHUNKS):
        rows = pl.ds(t * chunk, chunk)
        load_acts[t].wait()
        projected = jnp.dot(acts_v[rows, :], proj_v[...], preferred_element_type=F32)
        mine[rows, :] = projected.astype(BF16)
        summed[rows, :] = projected
        if t == 0:
            pl.semaphore_wait(barrier, 15)
        pair.append(send(mine.at[rows], theirs.at[rows], pair_send.at[t], pair_recv.at[t], sibling))
    for copy in load_moments:
        copy.wait()
    gather0 = [
        spread(0, half, 2, lambda m, half=half: moments.at[(half, *members[half])]) for half in range(2)
    ]
    for copy in load_grads:
        copy.wait()
    load_weight.start()
    for t in range(TOKEN_CHUNKS):
        rows = pl.ds(t * chunk, chunk)
        pair[t].wait_recv()
        both[:, t * chunk : (t + 1) * chunk] = (summed[rows, :] + theirs[rows, :].astype(F32)).T.astype(BF16)

    stage1 = []
    for half in range(2):
        block = jnp.dot(both[...], grads_v[half], preferred_element_type=F32).astype(BF16)
        for x in range(4):
            for y in range(4):
                for z in range(4):
                    row, column = x * 128 + y * 32 + z % 2 * 16, z // 2 * 128
                    at = [place(half, v) for v in (x, y, z)]
                    index = tuple(p[0] for p in at) + tuple(p[1] for p in at)
                    parts[(half, *index)] = block[row : row + 16, column : column + 128]
        stage1.append(
            spread(
                1,
                half,
                1,
                lambda m: parts.at[(half, *flip(sets[half], m))],
                lambda n: got1.at[half, n],
            )
        )

    stage2 = []
    for half in range(2):
        for copy in stage1[half]:
            copy.wait_recv()
        total = parts[(half, *sets[half])].astype(F32)
        for n in range(7):
            total += got1[half, n].astype(F32)
        own = (half, *members[half])
        sums[own] = total.astype(BF16)
        stage2.append(spread(2, half, 2, lambda m: sums.at[own]))

    gather2 = []
    for half in range(2):
        for copy in gather0[half]:
            copy.wait_recv()
        for copy in stage2[half]:
            copy.wait_recv()
        for i in range(2):
            for j in range(2):
                for k in range(2):
                    coefficients = sums[half, 0, 0, 0, i, j, k].astype(F32)
                    for n in range(1, 8):
                        coefficients += sums[(half, *bits(n), i, j, k)].astype(F32)
                    first_new = first_decay * moments[half, i, j, k, 0] + (1.0 - first_decay) * coefficients
                    second_new = (
                        second_decay * moments[half, i, j, k, 1]
                        + (1.0 - second_decay) * coefficients * coefficients
                    )
                    normalized = first_new / first_bias / (jnp.sqrt(second_new / second_bias) + epsilon)
                    gathered[(c, half, *sets[half], i, j, k)] = normalized.astype(BF16)
                    states[half, i, j, k, 0] = first_new
                    states[half, i, j, k, 1] = second_new
        gather2.append(spread(3, half, 1, lambda m: gathered.at[(c, half, *sets[half])]))
    for half in range(2):
        columns = slice(half * 128, (half + 1) * 128)
        first_new_ref[:, columns] = states[(half, *members[half], 0)]
        second_new_ref[:, columns] = states[(half, *members[half], 1)]

    forwards = []
    for far in range(2):
        for half in range(2):
            for n, m in enumerate(MASKS):
                if m // 4 == far:
                    gather2[half][n].wait_recv()
            x = sets[half][0]
            block = gathered.at[c, half, 1 - x if far else x]
            forwards.append(send(block, block, fw_send.at[half, far], fw_recv.at[half, far], sibling))
    for copy in forwards:
        copy.wait_recv()
    for copy in started:
        copy.wait_send()
    load_weight.wait()


def reduce_and_gather(*operands):
    proj, weight = operands[2], operands[3]
    vmem = pl.BlockSpec(memory_space=pltpu.VMEM)
    hbm = pl.BlockSpec(memory_space=pltpu.HBM)
    dma = pltpu.SemaphoreType.DMA
    return pl.pallas_call(
        reduce_kernel,
        out_shape=(
            pltpu.VMEM((2, 2, 2, 2, 2, 2, 2, 2, 16, 128), BF16),
            pltpu.VMEM(proj.shape, BF16),
            pltpu.VMEM(weight.shape, F32),
            pltpu.VMEM((16, 256), F32),
            pltpu.VMEM((16, 256), F32),
        ),
        in_specs=[hbm] * 6,
        out_specs=(vmem,) * 5,
        scratch_shapes=[
            pltpu.VMEM((512, 2048), BF16),
            pltpu.VMEM((2, 512, 256), BF16),
            pltpu.VMEM((512, 512), BF16),
            pltpu.VMEM((512, 512), BF16),
            pltpu.VMEM((512, 512), BF16),
            pltpu.VMEM((512, 512), F32),
            pltpu.VMEM((2, 2, 2, 2, 2, 2, 2, 16, 128), BF16),
            pltpu.VMEM((2, 7, 2, 2, 2, 16, 128), BF16),
            pltpu.VMEM((2, 2, 2, 2, 2, 2, 2, 16, 128), BF16),
            pltpu.VMEM((2, 2, 2, 2, 2, 16, 128), F32),
            pltpu.VMEM((2, 2, 2, 2, 2, 16, 128), F32),
            dma((10 + TOKEN_CHUNKS,)),
            dma((TOKEN_CHUNKS,)),
            dma((TOKEN_CHUNKS,)),
            dma((4, 2, 7)),
            dma((4, 2, 7)),
            dma((2, 2)),
            dma((2, 2)),
        ],
        compiler_params=pltpu.CompilerParams(
            collective_id=0, has_side_effects=True, vmem_limit_bytes=24 * 1024 * 1024
        ),
    )(*(pltpu.with_memory_space_constraint(a, pltpu.HBM) for a in operands))


def expand_kernel(
    gathered,
    proj,
    weight,
    first_in,
    second_in,
    new_weight,
    update,
    first_out,
    second_out,
    ordered,
    new_v,
    update_v,
    sems,
    state_sems,
):
    states = [
        pltpu.make_async_copy(first_in, first_out, state_sems.at[0]),
        pltpu.make_async_copy(second_in, second_out, state_sems.at[1]),
    ]
    for copy in states:
        copy.start()

    def stores(i):
        rows = pl.ds(i * ROW_TILE, ROW_TILE)
        return (
            pltpu.make_async_copy(new_v.at[rows], new_weight.at[rows], sems.at[0, i]),
            pltpu.make_async_copy(update_v.at[rows], update.at[rows], sems.at[1, i]),
        )

    for zh in range(2):
        for c in range(2):
            for half in range(2):
                column = zh * 512 + c * 256 + half * 128
                for x in range(4):
                    for y in range(4):
                        for zl in range(2):
                            at = [place(half, v) for v in (x, y, zh * 2 + zl)]
                            index = tuple(p[0] for p in at) + tuple(p[1] for p in at)
                            row = x * 128 + y * 32 + zl * 16
                            ordered[row : row + 16, column : column + 128] = gathered[(c, half, *index)]

    tiles = weight.shape[0] // ROW_TILE
    for i in range(tiles):
        rows = pl.ds(i * ROW_TILE, ROW_TILE)
        left = proj[rows, :]
        for n in range(4):
            columns = slice(n * 256, (n + 1) * 256)
            expanded = jnp.dot(left, ordered[:, columns], preferred_element_type=F32)
            new_v[rows, columns] = weight[rows, columns] - step_rate * expanded
            update_v[rows, columns] = expanded.astype(BF16)
        for copy in stores(i):
            copy.start()
    for i in range(tiles):
        for copy in stores(i):
            copy.wait()
    for copy in states:
        copy.wait()


def expand(gathered, proj, weight, first_new, second_new):
    depth, rank = proj.shape
    vmem = pl.BlockSpec(memory_space=pltpu.VMEM)
    hbm = pl.BlockSpec(memory_space=pltpu.HBM)
    return pl.pallas_call(
        expand_kernel,
        out_shape=(
            jax.ShapeDtypeStruct((depth, 1024), F32),
            jax.ShapeDtypeStruct((depth, 1024), BF16),
            jax.ShapeDtypeStruct((16, 256), F32),
            jax.ShapeDtypeStruct((16, 256), F32),
        ),
        in_specs=[vmem] * 5,
        out_specs=(hbm,) * 4,
        scratch_shapes=[
            pltpu.VMEM((rank, 1024), BF16),
            pltpu.VMEM((depth, 1024), F32),
            pltpu.VMEM((depth, 1024), BF16),
            pltpu.SemaphoreType.DMA((2, depth // ROW_TILE)),
            pltpu.SemaphoreType.DMA((2,)),
        ],
        compiler_params=pltpu.CompilerParams(vmem_limit_bytes=20 * 1024 * 1024),
    )(gathered, proj, weight, first_new, second_new)


def local(activations, out_grads, projector, weight, first_moment, second_moment):
    gathered, projector, weight, first_new, second_new = reduce_and_gather(
        activations, out_grads, projector, weight, first_moment, second_moment
    )
    return tuple(expand(gathered, projector, weight, first_new, second_new))


def solution(mesh):
    in_specs = (
        P("dp", "mp"),
        P("dp", None),
        P("mp", None),
        P("mp", None),
        P("dp", "mp"),
        P("dp", "mp"),
    )
    out_specs = (P("mp", None), P("mp", None), P("dp", "mp"), P("dp", "mp"))
    return jax.shard_map(local, mesh=mesh, in_specs=in_specs, out_specs=out_specs, check_vma=False)
```

```python
import functools

import jax
import jax.numpy as jnp
from jax import lax
from jax.experimental import pallas as pl
from jax.experimental.pallas import tpu as pltpu
from jax.sharding import PartitionSpec as P

first_decay = 0.9
second_decay = 0.999
first_bias = 1.0 - 0.9**2
second_bias = 1.0 - 0.999**2
epsilon = 1e-08
step_rate = 0.00025

MESH = pl.DeviceIdType.MESH
F32 = jnp.float32
BF16 = jnp.bfloat16
TOKEN_CHUNKS = 4
ROW_TILE = 256


def place(half, v):
    return ((v + v // 2) % 2, v // 2) if half == 0 else (v // 2, v % 2)


MASKS = (7, 6, 5, 3, 4, 2, 1)
PIECES = ((0, 0), (0, 1), (1, 0), (1, 1))


def bits(m):
    return m // 4, m // 2 % 2, m % 2


def reduce_kernel(
    acts,
    grads,
    proj,
    weight,
    first_moment,
    second_moment,
    gathered,
    proj_v,
    weight_v,
    first_new_ref,
    second_new_ref,
    acts_v,
    grads_v,
    mine,
    theirs,
    both,
    summed,
    parts,
    got1,
    sums,
    moments,
    states,
    load_sem,
    pair_send,
    pair_recv,
    send_sem,
    recv_sem,
    fw_send,
    fw_recv,
):
    dp = lax.axis_index("dp")
    mp = lax.axis_index("mp")
    zh, c = mp // 2, mp % 2
    chip = (dp // 8, (dp // 2) % 4, zh * 2 + dp % 2)
    sibling = (dp, zh * 2 + 1 - c)

    def partner(wrap, m):
        x, y, z = ((3 - v if wrap else v + 1 - 2 * (v % 2)) if bit else v for v, bit in zip(chip, bits(m)))
        return (x * 8 + y * 2 + z % 2, (z // 2) * 2 + c)

    def flip(at, m):
        return tuple(1 - v if bit else v for v, bit in zip(at, bits(m)))

    sets, members = [], []
    for half in range(2):
        places = [place(half, v) for v in chip]
        sets.append(tuple(p[0] for p in places))
        members.append(tuple(p[1] for p in places))

    tokens = acts.shape[0]
    chunk = tokens // TOKEN_CHUNKS
    load_proj = pltpu.make_async_copy(proj, proj_v, load_sem.at[0])
    load_proj.start()
    load_acts = []
    for t in range(TOKEN_CHUNKS):
        rows = pl.ds(t * chunk, chunk)
        copy = pltpu.make_async_copy(acts.at[rows], acts_v.at[rows], load_sem.at[1 + t])
        copy.start()
        load_acts.append(copy)
    load_grads = []
    for half in range(2):
        for h in range(2):
            columns = pl.ds(pl.multiple_of(h * 512 + c * 256 + half * 128, 128), 128)
            copy = pltpu.make_async_copy(
                grads.at[:, columns],
                grads_v.at[half, :, pl.ds(h * 128, 128)],
                load_sem.at[1 + TOKEN_CHUNKS + 2 * half + h],
            )
            copy.start()
            load_grads.append(copy)
    load_moments = []
    for half in range(2):
        columns = pl.ds(half * 128, 128)
        for n, moment in enumerate((first_moment, second_moment)):
            copy = pltpu.make_async_copy(
                moment.at[:, columns],
                moments.at[(half, *members[half], n)],
                load_sem.at[5 + TOKEN_CHUNKS + 2 * half + n],
            )
            copy.start()
            load_moments.append(copy)
    load_weight = pltpu.make_async_copy(weight, weight_v, load_sem.at[9 + TOKEN_CHUNKS])

    barrier = pltpu.get_barrier_semaphore()
    for device in [sibling] + [partner(wrap, m) for wrap in (False, True) for m in MASKS]:
        pl.semaphore_signal(barrier, inc=1, device_id=device, device_id_type=MESH)

    started = []

    def send(src, dst, sent, arrived, device):
        copy = pltpu.make_async_remote_copy(
            src_ref=src, dst_ref=dst, send_sem=sent, recv_sem=arrived, device_id=device, device_id_type=MESH
        )
        copy.start()
        started.append(copy)
        return copy

    def spread(stage, piece, half, flips, source, target=None):
        copies = []
        for n, m in enumerate(MASKS):
            src = source(m)
            dst = src if target is None else target(n)
            device = partner((half == 1) == (flips == 1), m)
            at = (stage, piece, half, n)
            copies.append(send(src, dst, send_sem.at[at], recv_sem.at[at], device))
        return copies

    def arrived(copies):
        for copy in copies:
            copy.wait_recv()

    load_proj.wait()
    pair = []
    for t in range(TOKEN_CHUNKS):
        rows = pl.ds(t * chunk, chunk)
        load_acts[t].wait()
        projected = jnp.dot(acts_v[rows, :], proj_v[...], preferred_element_type=F32)
        mine[rows, :] = projected.astype(BF16)
        summed[rows, :] = projected
        if t == 0:
            pl.semaphore_wait(barrier, 15)
        pair.append(send(mine.at[rows], theirs.at[rows], pair_send.at[t], pair_recv.at[t], sibling))
    for copy in load_moments:
        copy.wait()
    gather0 = [
        spread(0, 0, half, 2, lambda m, half=half: moments.at[(half, *members[half])]) for half in range(2)
    ]
    for copy in load_grads:
        copy.wait()
    load_weight.start()
    for t in range(TOKEN_CHUNKS):
        rows = pl.ds(t * chunk, chunk)
        pair[t].wait_recv()
        both[:, t * chunk : (t + 1) * chunk] = (summed[rows, :] + theirs[rows, :].astype(F32)).T.astype(BF16)

    stage1, stage2, gather2 = {}, {}, {}

    def scatter(piece, half):
        stage1[piece, half] = spread(
            1,
            piece,
            half,
            1,
            lambda m: parts.at[(half, *flip(sets[half], m), piece)],
            lambda n: got1.at[half, piece, n],
        )

    for half in range(2):
        block = jnp.dot(both[...], grads_v[half], preferred_element_type=F32).astype(BF16)
        for x in range(4):
            for y in range(4):
                for z in range(4):
                    row, column = x * 128 + y * 32 + z % 2 * 16, z // 2 * 128
                    at = [place(half, v) for v in (x, y, z)]
                    index = tuple(p[0] for p in at) + tuple(p[1] for p in at)
                    parts[(half, *index)] = block[row : row + 16, column : column + 128]
        scatter(0, half)
    scatter(1, 0)
    scatter(1, 1)

    for piece, half in PIECES:
        arrived(stage1[piece, half])
        total = parts[(half, *sets[half], piece)].astype(F32)
        for n in range(7):
            total += got1[half, piece, n].astype(F32)
        own = (half, *members[half], piece)
        sums[own] = total.astype(BF16)
        stage2[piece, half] = spread(2, piece, half, 2, lambda m: sums.at[own])

    for piece, half in PIECES:
        if piece == 0:
            arrived(gather0[half])
        arrived(stage2[piece, half])
        for j in range(2):
            for k in range(2):
                coefficients = sums[half, 0, 0, 0, piece, j, k].astype(F32)
                for n in range(1, 8):
                    coefficients += sums[(half, *bits(n), piece, j, k)].astype(F32)
                first_new = first_decay * moments[half, piece, j, k, 0] + (1.0 - first_decay) * coefficients
                second_new = (
                    second_decay * moments[half, piece, j, k, 1]
                    + (1.0 - second_decay) * coefficients * coefficients
                )
                normalized = first_new / first_bias / (jnp.sqrt(second_new / second_bias) + epsilon)
                gathered[(c, half, *sets[half], piece, j, k)] = normalized.astype(BF16)
                states[half, piece, j, k, 0] = first_new
                states[half, piece, j, k, 1] = second_new
        gather2[piece, half] = spread(3, piece, half, 1, lambda m: gathered.at[(c, half, *sets[half], piece)])
    for half in range(2):
        columns = slice(half * 128, (half + 1) * 128)
        first_new_ref[:, columns] = states[(half, *members[half], 0)]
        second_new_ref[:, columns] = states[(half, *members[half], 1)]

    forwards = []
    for piece, half in PIECES:
        arrived(gather2[piece, half])
        block = gathered.at[c, half, :, :, :, piece]
        forwards.append(send(block, block, fw_send.at[half, piece], fw_recv.at[half, piece], sibling))
    for copy in started:
        copy.wait_send()
    arrived(forwards)
    load_weight.wait()


def reduce_and_gather(*operands):
    proj, weight = operands[2], operands[3]
    vmem = pl.BlockSpec(memory_space=pltpu.VMEM)
    hbm = pl.BlockSpec(memory_space=pltpu.HBM)
    dma = pltpu.SemaphoreType.DMA
    return pl.pallas_call(
        reduce_kernel,
        out_shape=(
            pltpu.VMEM((2, 2, 2, 2, 2, 2, 2, 2, 16, 128), BF16),
            pltpu.VMEM(proj.shape, BF16),
            pltpu.VMEM(weight.shape, F32),
            pltpu.VMEM((16, 256), F32),
            pltpu.VMEM((16, 256), F32),
        ),
        in_specs=[hbm] * 6,
        out_specs=(vmem,) * 5,
        scratch_shapes=[
            pltpu.VMEM((512, 2048), BF16),
            pltpu.VMEM((2, 512, 256), BF16),
            pltpu.VMEM((512, 512), BF16),
            pltpu.VMEM((512, 512), BF16),
            pltpu.VMEM((512, 512), BF16),
            pltpu.VMEM((512, 512), F32),
            pltpu.VMEM((2, 2, 2, 2, 2, 2, 2, 16, 128), BF16),
            pltpu.VMEM((2, 2, 7, 2, 2, 16, 128), BF16),
            pltpu.VMEM((2, 2, 2, 2, 2, 2, 2, 16, 128), BF16),
            pltpu.VMEM((2, 2, 2, 2, 2, 16, 128), F32),
            pltpu.VMEM((2, 2, 2, 2, 2, 16, 128), F32),
            dma((10 + TOKEN_CHUNKS,)),
            dma((TOKEN_CHUNKS,)),
            dma((TOKEN_CHUNKS,)),
            dma((4, 2, 2, 7)),
            dma((4, 2, 2, 7)),
            dma((2, 2)),
            dma((2, 2)),
        ],
        compiler_params=pltpu.CompilerParams(
            collective_id=0, has_side_effects=True, vmem_limit_bytes=24 * 1024 * 1024
        ),
    )(*(pltpu.with_memory_space_constraint(a, pltpu.HBM) for a in operands))


def expand_kernel(
    gathered,
    proj,
    weight,
    first_in,
    second_in,
    new_weight,
    update,
    first_out,
    second_out,
    ordered,
    new_v,
    update_v,
    sems,
    state_sems,
):
    states = [
        pltpu.make_async_copy(first_in, first_out, state_sems.at[0]),
        pltpu.make_async_copy(second_in, second_out, state_sems.at[1]),
    ]
    for copy in states:
        copy.start()

    def stores(i):
        rows = pl.ds(i * ROW_TILE, ROW_TILE)
        return (
            pltpu.make_async_copy(new_v.at[rows], new_weight.at[rows], sems.at[0, i]),
            pltpu.make_async_copy(update_v.at[rows], update.at[rows], sems.at[1, i]),
        )

    for zh in range(2):
        for c in range(2):
            for half in range(2):
                column = zh * 512 + c * 256 + half * 128
                for x in range(4):
                    for y in range(4):
                        for zl in range(2):
                            at = [place(half, v) for v in (x, y, zh * 2 + zl)]
                            index = tuple(p[0] for p in at) + tuple(p[1] for p in at)
                            row = x * 128 + y * 32 + zl * 16
                            ordered[row : row + 16, column : column + 128] = gathered[(c, half, *index)]

    tiles = weight.shape[0] // ROW_TILE
    for i in range(tiles):
        rows = pl.ds(i * ROW_TILE, ROW_TILE)
        left = proj[rows, :]
        for n in range(4):
            columns = slice(n * 256, (n + 1) * 256)
            expanded = jnp.dot(left, ordered[:, columns], preferred_element_type=F32)
            new_v[rows, columns] = weight[rows, columns] - step_rate * expanded
            update_v[rows, columns] = expanded.astype(BF16)
        for copy in stores(i):
            copy.start()
    for i in range(tiles):
        for copy in stores(i):
            copy.wait()
    for copy in states:
        copy.wait()


def expand(gathered, proj, weight, first_new, second_new):
    depth, rank = proj.shape
    vmem = pl.BlockSpec(memory_space=pltpu.VMEM)
    hbm = pl.BlockSpec(memory_space=pltpu.HBM)
    return pl.pallas_call(
        expand_kernel,
        out_shape=(
            jax.ShapeDtypeStruct((depth, 1024), F32),
            jax.ShapeDtypeStruct((depth, 1024), BF16),
            jax.ShapeDtypeStruct((16, 256), F32),
            jax.ShapeDtypeStruct((16, 256), F32),
        ),
        in_specs=[vmem] * 5,
        out_specs=(hbm,) * 4,
        scratch_shapes=[
            pltpu.VMEM((rank, 1024), BF16),
            pltpu.VMEM((depth, 1024), F32),
            pltpu.VMEM((depth, 1024), BF16),
            pltpu.SemaphoreType.DMA((2, depth // ROW_TILE)),
            pltpu.SemaphoreType.DMA((2,)),
        ],
        compiler_params=pltpu.CompilerParams(vmem_limit_bytes=20 * 1024 * 1024),
    )(gathered, proj, weight, first_new, second_new)


def local(activations, out_grads, projector, weight, first_moment, second_moment):
    gathered, projector, weight, first_new, second_new = reduce_and_gather(
        activations, out_grads, projector, weight, first_moment, second_moment
    )
    return tuple(expand(gathered, projector, weight, first_new, second_new))


def solution(mesh):
    in_specs = (
        P("dp", "mp"),
        P("dp", None),
        P("mp", None),
        P("mp", None),
        P("dp", "mp"),
        P("dp", "mp"),
    )
    out_specs = (P("mp", None), P("mp", None), P("dp", "mp"), P("dp", "mp"))
    return jax.shard_map(local, mesh=mesh, in_specs=in_specs, out_specs=out_specs, check_vma=False)
```

```python
import functools

import jax
import jax.numpy as jnp
from jax import lax
from jax.experimental import pallas as pl
from jax.experimental.pallas import tpu as pltpu
from jax.sharding import PartitionSpec as P

first_decay = 0.9
second_decay = 0.999
first_bias = 1.0 - 0.9**2
second_bias = 1.0 - 0.999**2
epsilon = 1e-08
step_rate = 0.00025

MESH = pl.DeviceIdType.MESH
F32 = jnp.float32
BF16 = jnp.bfloat16
TOKEN_CHUNKS = 4
DEPTH_CHUNKS = 4
ROW_TILE = 256


WRAP_FIRST = ((False, False, True), (True, True, False))
HALVES = (1, 0)


def place(wrap_first, v):
    return (v // 2, v % 2) if wrap_first else ((v + v // 2) % 2, v // 2)


MASKS = (7, 6, 5, 3, 4, 2, 1)


def bits(m):
    return m // 4, m // 2 % 2, m % 2


def reduce_kernel(
    acts,
    grads,
    proj,
    weight,
    first_moment,
    second_moment,
    gathered,
    proj_v,
    weight_v,
    first_new_ref,
    second_new_ref,
    acts_v,
    grads_v,
    mine,
    theirs,
    both,
    summed,
    parts,
    got1,
    sums,
    moments,
    states,
    load_sem,
    pair_send,
    pair_recv,
    send_sem,
    recv_sem,
    fw_send,
    fw_recv,
):
    dp = lax.axis_index("dp")
    mp = lax.axis_index("mp")
    zh, c = mp // 2, mp % 2
    chip = (dp // 8, (dp // 2) % 4, zh * 2 + dp % 2)
    sibling = (dp, zh * 2 + 1 - c)

    terms = []
    for axis, v in enumerate(chip):
        options = (v, v + 1 - 2 * (v % 2), 3 - v)
        if axis == 2:
            terms.append([(o % 2, o // 2 * 2 + c) for o in options])
        else:
            terms.append([(o * (8, 2)[axis], 0) for o in options])

    def partner(half, flips, m):
        x, y, z = (
            terms[axis][(2 if WRAP_FIRST[half][axis] == (flips == 1) else 1) if bit else 0]
            for axis, bit in enumerate(bits(m))
        )
        return (x[0] + y[0] + z[0], z[1])

    def flip(at, m):
        return tuple(1 - v if bit else v for v, bit in zip(at, bits(m)))

    sets, members = [], []
    for half in range(2):
        places = [place(w, v) for w, v in zip(WRAP_FIRST[half], chip)]
        sets.append(tuple(p[0] for p in places))
        members.append(tuple(p[1] for p in places))

    tokens = acts.shape[0]
    chunk = tokens // TOKEN_CHUNKS
    depth = proj.shape[0] // DEPTH_CHUNKS
    load_proj, load_acts = [], []

    def load(loads, src, dst):
        copy = pltpu.make_async_copy(src, dst, load_sem.at[len(load_proj) + len(load_acts)])
        copy.start()
        loads.append(copy)

    for k in range(DEPTH_CHUNKS):
        rows = pl.ds(k * depth, depth)
        load(load_proj, proj.at[rows], proj_v.at[rows])
        if k == 0:
            load(load_acts, acts.at[pl.ds(0, chunk)], acts_v.at[pl.ds(0, chunk)])
    for t in range(1, TOKEN_CHUNKS):
        rows = pl.ds(t * chunk, chunk)
        load(load_acts, acts.at[rows], acts_v.at[rows])
    load_grads = []
    for half in range(2):
        for h in range(2):
            columns = pl.ds(pl.multiple_of(h * 512 + c * 256 + half * 128, 128), 128)
            copy = pltpu.make_async_copy(
                grads.at[:, columns],
                grads_v.at[half, :, pl.ds(h * 128, 128)],
                load_sem.at[DEPTH_CHUNKS + TOKEN_CHUNKS + 2 * half + h],
            )
            copy.start()
            load_grads.append(copy)
    load_moments = []
    for half in range(2):
        columns = pl.ds(half * 128, 128)
        for n, moment in enumerate((first_moment, second_moment)):
            copy = pltpu.make_async_copy(
                moment.at[:, columns],
                moments.at[(half, *members[half], n)],
                load_sem.at[4 + DEPTH_CHUNKS + TOKEN_CHUNKS + 2 * half + n],
            )
            copy.start()
            load_moments.append(copy)
    load_weight = pltpu.make_async_copy(weight, weight_v, load_sem.at[8 + DEPTH_CHUNKS + TOKEN_CHUNKS])

    barrier = pltpu.get_barrier_semaphore()
    for device in [sibling] + [partner(0, flips, m) for flips in (1, 2) for m in MASKS]:
        pl.semaphore_signal(barrier, inc=1, device_id=device, device_id_type=MESH)

    started = []

    def send(src, dst, sent, arrived, device):
        copy = pltpu.make_async_remote_copy(
            src_ref=src, dst_ref=dst, send_sem=sent, recv_sem=arrived, device_id=device, device_id_type=MESH
        )
        copy.start()
        started.append(copy)
        return copy

    def spread(stage, half, flips, source, target=None):
        copies = []
        for n, m in enumerate(MASKS):
            src = source(m)
            dst = src if target is None else target(n)
            device = partner(half, flips, m)
            copies.append(send(src, dst, send_sem.at[stage, half, n], recv_sem.at[stage, half, n], device))
        return copies

    pair = []
    for t in range(TOKEN_CHUNKS):
        rows = pl.ds(t * chunk, chunk)
        load_acts[t].wait()
        if t == 0:
            projected = jnp.zeros((chunk, proj.shape[1]), F32)
            for k in range(DEPTH_CHUNKS):
                at = pl.ds(k * depth, depth)
                load_proj[k].wait()
                projected += jnp.dot(acts_v[rows, at], proj_v[at, :], preferred_element_type=F32)
        else:
            projected = jnp.dot(acts_v[rows, :], proj_v[...], preferred_element_type=F32)
        mine[rows, :] = projected.astype(BF16)
        summed[rows, :] = projected
        if t == 0:
            pl.semaphore_wait(barrier, 15)
        pair.append(send(mine.at[rows], theirs.at[rows], pair_send.at[t], pair_recv.at[t], sibling))
    for copy in load_moments:
        copy.wait()
    gather0 = {}
    for half in HALVES:
        gather0[half] = spread(0, half, 2, lambda m: moments.at[(half, *members[half])])
    for copy in load_grads:
        copy.wait()
    load_weight.start()
    for t in range(TOKEN_CHUNKS):
        rows = pl.ds(t * chunk, chunk)
        pair[t].wait_recv()
        both[:, t * chunk : (t + 1) * chunk] = (summed[rows, :] + theirs[rows, :].astype(F32)).T.astype(BF16)

    stage1, stage2, gather2 = {}, {}, {}
    for half in HALVES:
        block = jnp.dot(both[...], grads_v[half], preferred_element_type=F32).astype(BF16)
        for x in range(4):
            for y in range(4):
                for z in range(4):
                    row, column = x * 128 + y * 32 + z % 2 * 16, z // 2 * 128
                    at = [place(w, v) for w, v in zip(WRAP_FIRST[half], (x, y, z))]
                    index = tuple(p[0] for p in at) + tuple(p[1] for p in at)
                    parts[(half, *index)] = block[row : row + 16, column : column + 128]
        stage1[half] = spread(
            1, half, 1, lambda m: parts.at[(half, *flip(sets[half], m))], lambda n: got1.at[half, n]
        )

    for half in HALVES:
        for copy in stage1[half]:
            copy.wait_recv()
        total = parts[(half, *sets[half])].astype(F32)
        for n in range(7):
            total += got1[half, n].astype(F32)
        own = (half, *members[half])
        sums[own] = total.astype(BF16)
        stage2[half] = spread(2, half, 2, lambda m: sums.at[own])

    for half in HALVES:
        for copy in gather0[half]:
            copy.wait_recv()
        for copy in stage2[half]:
            copy.wait_recv()
        for i in range(2):
            for j in range(2):
                for k in range(2):
                    coefficients = sums[half, 0, 0, 0, i, j, k].astype(F32)
                    for n in range(1, 8):
                        coefficients += sums[(half, *bits(n), i, j, k)].astype(F32)
                    first_new = first_decay * moments[half, i, j, k, 0] + (1.0 - first_decay) * coefficients
                    second_new = (
                        second_decay * moments[half, i, j, k, 1]
                        + (1.0 - second_decay) * coefficients * coefficients
                    )
                    normalized = first_new / first_bias / (jnp.sqrt(second_new / second_bias) + epsilon)
                    gathered[(c, half, *sets[half], i, j, k)] = normalized.astype(BF16)
                    states[half, i, j, k, 0] = first_new
                    states[half, i, j, k, 1] = second_new
        gather2[half] = spread(3, half, 1, lambda m: gathered.at[(c, half, *sets[half])])
    for half in range(2):
        columns = slice(half * 128, (half + 1) * 128)
        first_new_ref[:, columns] = states[(half, *members[half], 0)]
        second_new_ref[:, columns] = states[(half, *members[half], 1)]

    load_weight.wait()
    forwards = []
    for half in HALVES:
        for copy in gather2[half]:
            copy.wait_recv()
        block = gathered.at[c, half]
        forwards.append(send(block, block, fw_send.at[half], fw_recv.at[half], sibling))
    for copy in started:
        copy.wait_send()
    for copy in forwards:
        copy.wait_recv()


def reduce_and_gather(*operands):
    proj, weight = operands[2], operands[3]
    vmem = pl.BlockSpec(memory_space=pltpu.VMEM)
    hbm = pl.BlockSpec(memory_space=pltpu.HBM)
    dma = pltpu.SemaphoreType.DMA
    return pl.pallas_call(
        reduce_kernel,
        out_shape=(
            pltpu.VMEM((2, 2, 2, 2, 2, 2, 2, 2, 16, 128), BF16),
            pltpu.VMEM(proj.shape, BF16),
            pltpu.VMEM(weight.shape, F32),
            pltpu.VMEM((16, 256), F32),
            pltpu.VMEM((16, 256), F32),
        ),
        in_specs=[hbm] * 6,
        out_specs=(vmem,) * 5,
        scratch_shapes=[
            pltpu.VMEM((512, 2048), BF16),
            pltpu.VMEM((2, 512, 256), BF16),
            pltpu.VMEM((512, 512), BF16),
            pltpu.VMEM((512, 512), BF16),
            pltpu.VMEM((512, 512), BF16),
            pltpu.VMEM((512, 512), F32),
            pltpu.VMEM((2, 2, 2, 2, 2, 2, 2, 16, 128), BF16),
            pltpu.VMEM((2, 7, 2, 2, 2, 16, 128), BF16),
            pltpu.VMEM((2, 2, 2, 2, 2, 2, 2, 16, 128), BF16),
            pltpu.VMEM((2, 2, 2, 2, 2, 16, 128), F32),
            pltpu.VMEM((2, 2, 2, 2, 2, 16, 128), F32),
            dma((9 + DEPTH_CHUNKS + TOKEN_CHUNKS,)),
            dma((TOKEN_CHUNKS,)),
            dma((TOKEN_CHUNKS,)),
            dma((4, 2, 7)),
            dma((4, 2, 7)),
            dma((2,)),
            dma((2,)),
        ],
        compiler_params=pltpu.CompilerParams(
            collective_id=0, has_side_effects=True, vmem_limit_bytes=24 * 1024 * 1024
        ),
    )(*(pltpu.with_memory_space_constraint(a, pltpu.HBM) for a in operands))


def expand_kernel(
    gathered,
    proj,
    weight,
    first_in,
    second_in,
    new_weight,
    update,
    first_out,
    second_out,
    ordered,
    new_v,
    update_v,
    sems,
    state_sems,
):
    states = [
        pltpu.make_async_copy(first_in, first_out, state_sems.at[0]),
        pltpu.make_async_copy(second_in, second_out, state_sems.at[1]),
    ]
    for copy in states:
        copy.start()

    def stores(i):
        rows = pl.ds(i * ROW_TILE, ROW_TILE)
        return (
            pltpu.make_async_copy(new_v.at[rows], new_weight.at[rows], sems.at[0, i]),
            pltpu.make_async_copy(update_v.at[rows], update.at[rows], sems.at[1, i]),
        )

    for zh in range(2):
        for c in range(2):
            for half in range(2):
                column = zh * 512 + c * 256 + half * 128
                for x in range(4):
                    for y in range(4):
                        for zl in range(2):
                            at = [place(w, v) for w, v in zip(WRAP_FIRST[half], (x, y, zh * 2 + zl))]
                            index = tuple(p[0] for p in at) + tuple(p[1] for p in at)
                            row = x * 128 + y * 32 + zl * 16
                            ordered[row : row + 16, column : column + 128] = gathered[(c, half, *index)]

    tiles = weight.shape[0] // ROW_TILE
    for i in range(tiles):
        rows = pl.ds(i * ROW_TILE, ROW_TILE)
        left = proj[rows, :]
        for n in range(4):
            columns = slice(n * 256, (n + 1) * 256)
            expanded = jnp.dot(left, ordered[:, columns], preferred_element_type=F32)
            new_v[rows, columns] = weight[rows, columns] - step_rate * expanded
            update_v[rows, columns] = expanded.astype(BF16)
        for copy in stores(i):
            copy.start()
    for i in range(tiles):
        for copy in stores(i):
            copy.wait()
    for copy in states:
        copy.wait()


def expand(gathered, proj, weight, first_new, second_new):
    depth, rank = proj.shape
    vmem = pl.BlockSpec(memory_space=pltpu.VMEM)
    hbm = pl.BlockSpec(memory_space=pltpu.HBM)
    return pl.pallas_call(
        expand_kernel,
        out_shape=(
            jax.ShapeDtypeStruct((depth, 1024), F32),
            jax.ShapeDtypeStruct((depth, 1024), BF16),
            jax.ShapeDtypeStruct((16, 256), F32),
            jax.ShapeDtypeStruct((16, 256), F32),
        ),
        in_specs=[vmem] * 5,
        out_specs=(hbm,) * 4,
        scratch_shapes=[
            pltpu.VMEM((rank, 1024), BF16),
            pltpu.VMEM((depth, 1024), F32),
            pltpu.VMEM((depth, 1024), BF16),
            pltpu.SemaphoreType.DMA((2, depth // ROW_TILE)),
            pltpu.SemaphoreType.DMA((2,)),
        ],
        compiler_params=pltpu.CompilerParams(vmem_limit_bytes=20 * 1024 * 1024),
    )(gathered, proj, weight, first_new, second_new)


def local(activations, out_grads, projector, weight, first_moment, second_moment):
    gathered, projector, weight, first_new, second_new = reduce_and_gather(
        activations, out_grads, projector, weight, first_moment, second_moment
    )
    return tuple(expand(gathered, projector, weight, first_new, second_new))


def solution(mesh):
    in_specs = (
        P("dp", "mp"),
        P("dp", None),
        P("mp", None),
        P("mp", None),
        P("dp", "mp"),
        P("dp", "mp"),
    )
    out_specs = (P("mp", None), P("mp", None), P("dp", "mp"), P("dp", "mp"))
    return jax.shard_map(local, mesh=mesh, in_specs=in_specs, out_specs=out_specs, check_vma=False)
```

```python
import functools

import jax
import jax.numpy as jnp
from jax import lax
from jax.experimental import pallas as pl
from jax.experimental.pallas import tpu as pltpu
from jax.sharding import PartitionSpec as P

first_decay = 0.9
second_decay = 0.999
first_bias = 1.0 - 0.9**2
second_bias = 1.0 - 0.999**2
epsilon = 1e-08
step_rate = 0.00025

MESH = pl.DeviceIdType.MESH
F32 = jnp.float32
BF16 = jnp.bfloat16
TOKEN_BLOCKS = 4
DEPTH_PARTS = 8
ROW_TILE = 256


WRAP_FIRST = ((False, False, True), (True, True, False))
HALVES = (1, 0)


def place(wrap_first, v):
    return (v // 2, v % 2) if wrap_first else ((v + v // 2) % 2, v // 2)


MASKS = (7, 6, 5, 3, 4, 2, 1)


def bits(m):
    return m // 4, m // 2 % 2, m % 2


def reduce_kernel(
    acts,
    grads,
    proj,
    weight,
    first_moment,
    second_moment,
    gathered,
    proj_v,
    weight_v,
    first_new_ref,
    second_new_ref,
    acts_v,
    grads_v,
    mine,
    theirs,
    both,
    summed,
    parts,
    got1,
    sums,
    moments,
    states,
    load_sem,
    pair_send,
    pair_recv,
    send_sem,
    recv_sem,
    fw_send,
    fw_recv,
):
    dp = lax.axis_index("dp")
    mp = lax.axis_index("mp")
    zh, c = mp // 2, mp % 2
    chip = (dp // 8, (dp // 2) % 4, zh * 2 + dp % 2)
    sibling = (dp, zh * 2 + 1 - c)

    terms = []
    for axis, v in enumerate(chip):
        options = (v, v + 1 - 2 * (v % 2), 3 - v)
        if axis == 2:
            terms.append([(o % 2, o // 2 * 2 + c) for o in options])
        else:
            terms.append([(o * (8, 2)[axis], 0) for o in options])

    def partner(half, flips, m):
        x, y, z = (
            terms[axis][(2 if WRAP_FIRST[half][axis] == (flips == 1) else 1) if bit else 0]
            for axis, bit in enumerate(bits(m))
        )
        return (x[0] + y[0] + z[0], z[1])

    def flip(at, m):
        return tuple(1 - v if bit else v for v, bit in zip(at, bits(m)))

    sets, members = [], []
    for half in range(2):
        places = [place(w, v) for w, v in zip(WRAP_FIRST[half], chip)]
        sets.append(tuple(p[0] for p in places))
        members.append(tuple(p[1] for p in places))

    depth = proj.shape[0] // DEPTH_PARTS
    load_parts = []

    def load_part(k):
        at = pl.ds(k * depth, depth)
        for n, (src, dst) in enumerate(((proj.at[at], proj_v.at[at]), (acts.at[:, at], acts_v.at[:, at]))):
            copy = pltpu.make_async_copy(src, dst, load_sem.at[2 * k + n])
            copy.start()
            load_parts.append(copy)

    load_part(0)
    barrier = pltpu.get_barrier_semaphore()
    for device in [sibling] + [partner(0, flips, m) for flips in (1, 2) for m in MASKS]:
        pl.semaphore_signal(barrier, inc=1, device_id=device, device_id_type=MESH)
    for k in range(1, DEPTH_PARTS):
        load_part(k)
    load_grads = []
    for half in range(2):
        for h in range(2):
            columns = pl.ds(pl.multiple_of(h * 512 + c * 256 + half * 128, 128), 128)
            copy = pltpu.make_async_copy(
                grads.at[:, columns],
                grads_v.at[half, :, pl.ds(h * 128, 128)],
                load_sem.at[2 * DEPTH_PARTS + 2 * half + h],
            )
            copy.start()
            load_grads.append(copy)
    load_moments = []
    for half in range(2):
        columns = pl.ds(half * 128, 128)
        for n, moment in enumerate((first_moment, second_moment)):
            copy = pltpu.make_async_copy(
                moment.at[:, columns],
                moments.at[(half, *members[half], n)],
                load_sem.at[4 + 2 * DEPTH_PARTS + 2 * half + n],
            )
            copy.start()
            load_moments.append(copy)
    load_weight = pltpu.make_async_copy(weight, weight_v, load_sem.at[8 + 2 * DEPTH_PARTS])

    started = []

    def send(src, dst, sent, arrived, device):
        copy = pltpu.make_async_remote_copy(
            src_ref=src, dst_ref=dst, send_sem=sent, recv_sem=arrived, device_id=device, device_id_type=MESH
        )
        copy.start()
        started.append(copy)
        return copy

    def spread(stage, half, flips, source, target=None):
        copies = []
        for n, m in enumerate(MASKS):
            src = source(m)
            dst = src if target is None else target(n)
            device = partner(half, flips, m)
            copies.append(send(src, dst, send_sem.at[stage, half, n], recv_sem.at[stage, half, n], device))
        return copies

    for k in range(DEPTH_PARTS):
        at = pl.ds(k * depth, depth)
        load_parts[2 * k].wait()
        load_parts[2 * k + 1].wait()
        product = jnp.dot(acts_v[:, at], proj_v[at, :], preferred_element_type=F32)
        projected = product if k == 0 else projected + product
    block = projected.shape[0] // TOKEN_BLOCKS
    for t in range(TOKEN_BLOCKS):
        turned = projected[t * block : (t + 1) * block].T
        summed[t] = turned
        mine[t] = turned.astype(BF16)
    pl.semaphore_wait(barrier, 15)
    pair = [send(mine.at[t], theirs.at[t], pair_send.at[t], pair_recv.at[t], sibling) for t in range(TOKEN_BLOCKS)]
    for copy in load_grads:
        copy.wait()
    load_weight.start()
    for t in range(TOKEN_BLOCKS):
        pair[t].wait_recv()
        both[:, t * block : (t + 1) * block] = (summed[t] + theirs[t].astype(F32)).astype(BF16)

    stage1, stage2, gather2 = {}, {}, {}
    for half in HALVES:
        product = jnp.dot(both[...], grads_v[half], preferred_element_type=F32).astype(BF16)
        for x in range(4):
            for y in range(4):
                for z in range(4):
                    row, column = x * 128 + y * 32 + z % 2 * 16, z // 2 * 128
                    at = [place(w, v) for w, v in zip(WRAP_FIRST[half], (x, y, z))]
                    index = tuple(p[0] for p in at) + tuple(p[1] for p in at)
                    parts[(half, *index)] = product[row : row + 16, column : column + 128]
        stage1[half] = spread(
            1, half, 1, lambda m: parts.at[(half, *flip(sets[half], m))], lambda n: got1.at[half, n]
        )

    for copy in load_moments:
        copy.wait()
    gather0 = {}
    for half in HALVES:
        gather0[half] = spread(0, half, 2, lambda m: moments.at[(half, *members[half])])

    for half in HALVES:
        for copy in stage1[half]:
            copy.wait_recv()
        total = parts[(half, *sets[half])].astype(F32)
        for n in range(7):
            total += got1[half, n].astype(F32)
        own = (half, *members[half])
        sums[own] = total.astype(BF16)
        stage2[half] = spread(2, half, 2, lambda m: sums.at[own])

    for half in HALVES:
        for copy in gather0[half]:
            copy.wait_recv()
        for copy in stage2[half]:
            copy.wait_recv()
        for i in range(2):
            for j in range(2):
                for k in range(2):
                    coefficients = sums[half, 0, 0, 0, i, j, k].astype(F32)
                    for n in range(1, 8):
                        coefficients += sums[(half, *bits(n), i, j, k)].astype(F32)
                    first_new = first_decay * moments[half, i, j, k, 0] + (1.0 - first_decay) * coefficients
                    second_new = (
                        second_decay * moments[half, i, j, k, 1]
                        + (1.0 - second_decay) * coefficients * coefficients
                    )
                    normalized = first_new / first_bias / (jnp.sqrt(second_new / second_bias) + epsilon)
                    gathered[(c, half, *sets[half], i, j, k)] = normalized.astype(BF16)
                    states[half, i, j, k, 0] = first_new
                    states[half, i, j, k, 1] = second_new
        gather2[half] = spread(3, half, 1, lambda m: gathered.at[(c, half, *sets[half])])
    for half in range(2):
        columns = slice(half * 128, (half + 1) * 128)
        first_new_ref[:, columns] = states[(half, *members[half], 0)]
        second_new_ref[:, columns] = states[(half, *members[half], 1)]

    load_weight.wait()
    forwards = []
    for half in HALVES:
        for copy in gather2[half]:
            copy.wait_recv()
        block = gathered.at[c, half]
        forwards.append(send(block, block, fw_send.at[half], fw_recv.at[half], sibling))
    for copy in started:
        copy.wait_send()
    for copy in forwards:
        copy.wait_recv()


def reduce_and_gather(*operands):
    proj, weight = operands[2], operands[3]
    vmem = pl.BlockSpec(memory_space=pltpu.VMEM)
    hbm = pl.BlockSpec(memory_space=pltpu.HBM)
    dma = pltpu.SemaphoreType.DMA
    return pl.pallas_call(
        reduce_kernel,
        out_shape=(
            pltpu.VMEM((2, 2, 2, 2, 2, 2, 2, 2, 16, 128), BF16),
            pltpu.VMEM(proj.shape, BF16),
            pltpu.VMEM(weight.shape, F32),
            pltpu.VMEM((16, 256), F32),
            pltpu.VMEM((16, 256), F32),
        ),
        in_specs=[hbm] * 6,
        out_specs=(vmem,) * 5,
        scratch_shapes=[
            pltpu.VMEM((512, 2048), BF16),
            pltpu.VMEM((2, 512, 256), BF16),
            pltpu.VMEM((TOKEN_BLOCKS, 512, 512 // TOKEN_BLOCKS), BF16),
            pltpu.VMEM((TOKEN_BLOCKS, 512, 512 // TOKEN_BLOCKS), BF16),
            pltpu.VMEM((512, 512), BF16),
            pltpu.VMEM((TOKEN_BLOCKS, 512, 512 // TOKEN_BLOCKS), F32),
            pltpu.VMEM((2, 2, 2, 2, 2, 2, 2, 16, 128), BF16),
            pltpu.VMEM((2, 7, 2, 2, 2, 16, 128), BF16),
            pltpu.VMEM((2, 2, 2, 2, 2, 2, 2, 16, 128), BF16),
            pltpu.VMEM((2, 2, 2, 2, 2, 16, 128), F32),
            pltpu.VMEM((2, 2, 2, 2, 2, 16, 128), F32),
            dma((9 + 2 * DEPTH_PARTS,)),
            dma((TOKEN_BLOCKS,)),
            dma((TOKEN_BLOCKS,)),
            dma((4, 2, 7)),
            dma((4, 2, 7)),
            dma((2,)),
            dma((2,)),
        ],
        compiler_params=pltpu.CompilerParams(
            collective_id=0, has_side_effects=True, vmem_limit_bytes=24 * 1024 * 1024
        ),
    )(*(pltpu.with_memory_space_constraint(a, pltpu.HBM) for a in operands))


def expand_kernel(
    gathered,
    proj,
    weight,
    first_in,
    second_in,
    new_weight,
    update,
    first_out,
    second_out,
    ordered,
    new_v,
    update_v,
    sems,
    state_sems,
):
    states = [
        pltpu.make_async_copy(first_in, first_out, state_sems.at[0]),
        pltpu.make_async_copy(second_in, second_out, state_sems.at[1]),
    ]
    for copy in states:
        copy.start()

    def stores(i):
        rows = pl.ds(i * ROW_TILE, ROW_TILE)
        return (
            pltpu.make_async_copy(new_v.at[rows], new_weight.at[rows], sems.at[0, i]),
            pltpu.make_async_copy(update_v.at[rows], update.at[rows], sems.at[1, i]),
        )

    for zh in range(2):
        for c in range(2):
            for half in range(2):
                column = zh * 512 + c * 256 + half * 128
                for x in range(4):
                    for y in range(4):
                        for zl in range(2):
                            at = [place(w, v) for w, v in zip(WRAP_FIRST[half], (x, y, zh * 2 + zl))]
                            index = tuple(p[0] for p in at) + tuple(p[1] for p in at)
                            row = x * 128 + y * 32 + zl * 16
                            ordered[row : row + 16, column : column + 128] = gathered[(c, half, *index)]

    tiles = weight.shape[0] // ROW_TILE
    for i in range(tiles):
        rows = pl.ds(i * ROW_TILE, ROW_TILE)
        left = proj[rows, :]
        for n in range(4):
            columns = slice(n * 256, (n + 1) * 256)
            expanded = jnp.dot(left, ordered[:, columns], preferred_element_type=F32)
            new_v[rows, columns] = weight[rows, columns] - step_rate * expanded
            update_v[rows, columns] = expanded.astype(BF16)
        for copy in stores(i):
            copy.start()
    for i in range(tiles):
        for copy in stores(i):
            copy.wait()
    for copy in states:
        copy.wait()


def expand(gathered, proj, weight, first_new, second_new):
    depth, rank = proj.shape
    vmem = pl.BlockSpec(memory_space=pltpu.VMEM)
    hbm = pl.BlockSpec(memory_space=pltpu.HBM)
    return pl.pallas_call(
        expand_kernel,
        out_shape=(
            jax.ShapeDtypeStruct((depth, 1024), F32),
            jax.ShapeDtypeStruct((depth, 1024), BF16),
            jax.ShapeDtypeStruct((16, 256), F32),
            jax.ShapeDtypeStruct((16, 256), F32),
        ),
        in_specs=[vmem] * 5,
        out_specs=(hbm,) * 4,
        scratch_shapes=[
            pltpu.VMEM((rank, 1024), BF16),
            pltpu.VMEM((depth, 1024), F32),
            pltpu.VMEM((depth, 1024), BF16),
            pltpu.SemaphoreType.DMA((2, depth // ROW_TILE)),
            pltpu.SemaphoreType.DMA((2,)),
        ],
        compiler_params=pltpu.CompilerParams(vmem_limit_bytes=20 * 1024 * 1024),
    )(gathered, proj, weight, first_new, second_new)


def local(activations, out_grads, projector, weight, first_moment, second_moment):
    gathered, projector, weight, first_new, second_new = reduce_and_gather(
        activations, out_grads, projector, weight, first_moment, second_moment
    )
    return tuple(expand(gathered, projector, weight, first_new, second_new))


def solution(mesh):
    in_specs = (
        P("dp", "mp"),
        P("dp", None),
        P("mp", None),
        P("mp", None),
        P("dp", "mp"),
        P("dp", "mp"),
    )
    out_specs = (P("mp", None), P("mp", None), P("dp", "mp"), P("dp", "mp"))
    return jax.shard_map(local, mesh=mesh, in_specs=in_specs, out_specs=out_specs, check_vma=False)
```

```python
import functools

import jax
import jax.numpy as jnp
from jax import lax
from jax.experimental import pallas as pl
from jax.experimental.pallas import tpu as pltpu
from jax.sharding import PartitionSpec as P

first_decay = 0.9
second_decay = 0.999
first_bias = 1.0 - 0.9**2
second_bias = 1.0 - 0.999**2
epsilon = 1e-08
step_rate = 0.00025

MESH = pl.DeviceIdType.MESH
F32 = jnp.float32
BF16 = jnp.bfloat16
TOKEN_BLOCKS = 4
DEPTH_PARTS = 8
ROW_TILE = 512


WRAP_FIRST = ((False, False, True), (True, True, False))
HALVES = (1, 0)


def place(wrap_first, v):
    return (v // 2, v % 2) if wrap_first else ((v + v // 2) % 2, v // 2)


MASKS = (7, 6, 5, 3, 4, 2, 1)


def bits(m):
    return m // 4, m // 2 % 2, m % 2


def reduce_kernel(
    acts,
    grads,
    proj,
    weight,
    first_moment,
    second_moment,
    other,
    own_new,
    own_update,
    proj_v,
    weight_v,
    first_new_ref,
    second_new_ref,
    gathered,
    own,
    acts_v,
    grads_v,
    mine,
    theirs,
    both,
    summed,
    parts,
    got1,
    sums,
    moments,
    states,
    load_sem,
    pair_send,
    pair_recv,
    send_sem,
    recv_sem,
    fw_send,
    fw_recv,
):
    dp = lax.axis_index("dp")
    mp = lax.axis_index("mp")
    zh, c = mp // 2, mp % 2
    chip = (dp // 8, (dp // 2) % 4, zh * 2 + dp % 2)
    sibling = (dp, zh * 2 + 1 - c)

    terms = []
    for axis, v in enumerate(chip):
        options = (v, v + 1 - 2 * (v % 2), 3 - v)
        if axis == 2:
            terms.append([(o % 2, o // 2 * 2 + c) for o in options])
        else:
            terms.append([(o * (8, 2)[axis], 0) for o in options])

    def partner(half, flips, m):
        x, y, z = (
            terms[axis][(2 if WRAP_FIRST[half][axis] == (flips == 1) else 1) if bit else 0]
            for axis, bit in enumerate(bits(m))
        )
        return (x[0] + y[0] + z[0], z[1])

    def flip(at, m):
        return tuple(1 - v if bit else v for v, bit in zip(at, bits(m)))

    sets, members = [], []
    for half in range(2):
        places = [place(w, v) for w, v in zip(WRAP_FIRST[half], chip)]
        sets.append(tuple(p[0] for p in places))
        members.append(tuple(p[1] for p in places))

    depth = proj.shape[0] // DEPTH_PARTS
    load_parts = []

    def load_part(k):
        at = pl.ds(k * depth, depth)
        for n, (src, dst) in enumerate(((proj.at[at], proj_v.at[at]), (acts.at[:, at], acts_v.at[:, at]))):
            copy = pltpu.make_async_copy(src, dst, load_sem.at[2 * k + n])
            copy.start()
            load_parts.append(copy)

    load_part(0)
    barrier = pltpu.get_barrier_semaphore()
    for device in [sibling] + [partner(0, flips, m) for flips in (1, 2) for m in MASKS]:
        pl.semaphore_signal(barrier, inc=1, device_id=device, device_id_type=MESH)
    for k in range(1, DEPTH_PARTS):
        load_part(k)
    load_grads = []
    for half in range(2):
        for h in range(2):
            columns = pl.ds(pl.multiple_of(h * 512 + c * 256 + half * 128, 128), 128)
            copy = pltpu.make_async_copy(
                grads.at[:, columns],
                grads_v.at[half, :, pl.ds(h * 128, 128)],
                load_sem.at[2 * DEPTH_PARTS + 2 * half + h],
            )
            copy.start()
            load_grads.append(copy)
    load_moments = []
    for half in range(2):
        columns = pl.ds(half * 128, 128)
        for n, moment in enumerate((first_moment, second_moment)):
            copy = pltpu.make_async_copy(
                moment.at[:, columns],
                moments.at[(half, *members[half], n)],
                load_sem.at[4 + 2 * DEPTH_PARTS + 2 * half + n],
            )
            copy.start()
            load_moments.append(copy)
    load_weight = pltpu.make_async_copy(weight, weight_v, load_sem.at[8 + 2 * DEPTH_PARTS])

    started = []

    def send(src, dst, sent, arrived, device):
        copy = pltpu.make_async_remote_copy(
            src_ref=src, dst_ref=dst, send_sem=sent, recv_sem=arrived, device_id=device, device_id_type=MESH
        )
        copy.start()
        started.append(copy)
        return copy

    def spread(stage, half, flips, source, target=None):
        copies = []
        for n, m in enumerate(MASKS):
            src = source(m)
            dst = src if target is None else target(n)
            device = partner(half, flips, m)
            copies.append(send(src, dst, send_sem.at[stage, half, n], recv_sem.at[stage, half, n], device))
        return copies

    for k in range(DEPTH_PARTS):
        at = pl.ds(k * depth, depth)
        load_parts[2 * k].wait()
        load_parts[2 * k + 1].wait()
        product = jnp.dot(acts_v[:, at], proj_v[at, :], preferred_element_type=F32)
        projected = product if k == 0 else projected + product
    block = projected.shape[0] // TOKEN_BLOCKS
    for t in range(TOKEN_BLOCKS):
        turned = projected[t * block : (t + 1) * block].T
        summed[t] = turned
        mine[t] = turned.astype(BF16)
    pl.semaphore_wait(barrier, 15)
    pair = [send(mine.at[t], theirs.at[t], pair_send.at[t], pair_recv.at[t], sibling) for t in range(TOKEN_BLOCKS)]
    for copy in load_grads:
        copy.wait()
    load_weight.start()
    for t in range(TOKEN_BLOCKS):
        pair[t].wait_recv()
        both[:, t * block : (t + 1) * block] = (summed[t] + theirs[t].astype(F32)).astype(BF16)

    stage1, stage2, gather2 = {}, {}, {}
    for half in HALVES:
        product = jnp.dot(both[...], grads_v[half], preferred_element_type=F32).astype(BF16)
        for x in range(4):
            for y in range(4):
                for z in range(4):
                    row, column = x * 128 + y * 32 + z % 2 * 16, z // 2 * 128
                    at = [place(w, v) for w, v in zip(WRAP_FIRST[half], (x, y, z))]
                    index = tuple(p[0] for p in at) + tuple(p[1] for p in at)
                    parts[(half, *index)] = product[row : row + 16, column : column + 128]
        stage1[half] = spread(
            1, half, 1, lambda m: parts.at[(half, *flip(sets[half], m))], lambda n: got1.at[half, n]
        )

    for copy in load_moments:
        copy.wait()
    gather0 = {}
    for half in HALVES:
        gather0[half] = spread(0, half, 2, lambda m: moments.at[(half, *members[half])])

    for half in HALVES:
        for copy in stage1[half]:
            copy.wait_recv()
        total = parts[(half, *sets[half])].astype(F32)
        for n in range(7):
            total += got1[half, n].astype(F32)
        here = (half, *members[half])
        sums[here] = total.astype(BF16)
        stage2[half] = spread(2, half, 2, lambda m: sums.at[here])

    for half in HALVES:
        for copy in gather0[half]:
            copy.wait_recv()
        for copy in stage2[half]:
            copy.wait_recv()
        for i in range(2):
            for j in range(2):
                for k in range(2):
                    coefficients = sums[half, 0, 0, 0, i, j, k].astype(F32)
                    for n in range(1, 8):
                        coefficients += sums[(half, *bits(n), i, j, k)].astype(F32)
                    first_new = first_decay * moments[half, i, j, k, 0] + (1.0 - first_decay) * coefficients
                    second_new = (
                        second_decay * moments[half, i, j, k, 1]
                        + (1.0 - second_decay) * coefficients * coefficients
                    )
                    normalized = first_new / first_bias / (jnp.sqrt(second_new / second_bias) + epsilon)
                    gathered[(c, half, *sets[half], i, j, k)] = normalized.astype(BF16)
                    states[half, i, j, k, 0] = first_new
                    states[half, i, j, k, 1] = second_new
        gather2[half] = spread(3, half, 1, lambda m: gathered.at[(c, half, *sets[half])])
    for half in range(2):
        columns = slice(half * 128, (half + 1) * 128)
        first_new_ref[:, columns] = states[(half, *members[half], 0)]
        second_new_ref[:, columns] = states[(half, *members[half], 1)]

    forwards = {}
    for half in HALVES:
        for copy in gather2[half]:
            copy.wait_recv()
        block = gathered.at[c, half]
        forwards[half] = send(block, block, fw_send.at[half], fw_recv.at[half], sibling)

    def order(core, half, target):
        for x in range(4):
            for y in range(4):
                for z in range(4):
                    row, column = x * 128 + y * 32 + z % 2 * 16, z // 2 * 256 + half * 128
                    at = [place(w, v) for w, v in zip(WRAP_FIRST[half], (x, y, z))]
                    index = tuple(p[0] for p in at) + tuple(p[1] for p in at)
                    target[row : row + 16, column : column + 128] = gathered[(core, half, *index)]

    for half in HALVES:
        order(c, half, own)
    load_weight.wait()
    for rows, columns, here in column_tiles(weight_v.shape[0], c):
        expanded = jnp.dot(proj_v[rows, :], own[:, columns], preferred_element_type=F32)
        own_new[rows, columns] = weight_v[rows, here] - step_rate * expanded
        own_update[rows, columns] = expanded.astype(BF16)

    for copy in started:
        copy.wait_send()
    for half in HALVES:
        forwards[half].wait_recv()
        order(1 - c, half, other)


def column_tiles(depth, core):
    for h in range(2):
        for i in range(depth // ROW_TILE):
            rows = pl.ds(i * ROW_TILE, ROW_TILE)
            yield rows, pl.ds(h * 256, 256), pl.ds(pl.multiple_of(h * 512 + core * 256, 256), 256)


def reduce_and_gather(*operands):
    proj, weight = operands[2], operands[3]
    vmem = pl.BlockSpec(memory_space=pltpu.VMEM)
    hbm = pl.BlockSpec(memory_space=pltpu.HBM)
    dma = pltpu.SemaphoreType.DMA
    return pl.pallas_call(
        reduce_kernel,
        out_shape=(
            pltpu.VMEM((512, 512), BF16),
            pltpu.VMEM((proj.shape[0], 512), F32),
            pltpu.VMEM((proj.shape[0], 512), BF16),
            pltpu.VMEM(proj.shape, BF16),
            pltpu.VMEM(weight.shape, F32),
            pltpu.VMEM((16, 256), F32),
            pltpu.VMEM((16, 256), F32),
        ),
        in_specs=[hbm] * 6,
        out_specs=(vmem,) * 7,
        scratch_shapes=[
            pltpu.VMEM((2, 2, 2, 2, 2, 2, 2, 2, 16, 128), BF16),
            pltpu.VMEM((512, 512), BF16),
            pltpu.VMEM((512, 2048), BF16),
            pltpu.VMEM((2, 512, 256), BF16),
            pltpu.VMEM((TOKEN_BLOCKS, 512, 512 // TOKEN_BLOCKS), BF16),
            pltpu.VMEM((TOKEN_BLOCKS, 512, 512 // TOKEN_BLOCKS), BF16),
            pltpu.VMEM((512, 512), BF16),
            pltpu.VMEM((TOKEN_BLOCKS, 512, 512 // TOKEN_BLOCKS), F32),
            pltpu.VMEM((2, 2, 2, 2, 2, 2, 2, 16, 128), BF16),
            pltpu.VMEM((2, 7, 2, 2, 2, 16, 128), BF16),
            pltpu.VMEM((2, 2, 2, 2, 2, 2, 2, 16, 128), BF16),
            pltpu.VMEM((2, 2, 2, 2, 2, 16, 128), F32),
            pltpu.VMEM((2, 2, 2, 2, 2, 16, 128), F32),
            dma((9 + 2 * DEPTH_PARTS,)),
            dma((TOKEN_BLOCKS,)),
            dma((TOKEN_BLOCKS,)),
            dma((4, 2, 7)),
            dma((4, 2, 7)),
            dma((2,)),
            dma((2,)),
        ],
        compiler_params=pltpu.CompilerParams(
            collective_id=0, has_side_effects=True, vmem_limit_bytes=24 * 1024 * 1024
        ),
    )(*(pltpu.with_memory_space_constraint(a, pltpu.HBM) for a in operands))


def expand_kernel(
    other,
    own_new,
    own_update,
    proj,
    weight,
    first_in,
    second_in,
    new_weight,
    update,
    first_out,
    second_out,
    new_v,
    update_v,
    sems,
    state_sems,
):
    c = lax.axis_index("mp") % 2
    copies = [
        pltpu.make_async_copy(first_in, first_out, state_sems.at[0]),
        pltpu.make_async_copy(second_in, second_out, state_sems.at[1]),
    ]
    for copy in copies:
        copy.start()

    def store(new, upd, core, i, rows, columns, here):
        for n, (src, dst) in enumerate(((new, new_weight), (upd, update))):
            copy = pltpu.make_async_copy(src.at[rows, columns], dst.at[rows, here], sems.at[core, n, i])
            copy.start()
            copies.append(copy)

    depth = weight.shape[0]
    for i, at in enumerate(column_tiles(depth, c)):
        store(own_new, own_update, 0, i, *at)
    for i, (rows, columns, here) in enumerate(column_tiles(depth, 1 - c)):
        expanded = jnp.dot(proj[rows, :], other[:, columns], preferred_element_type=F32)
        new_v[rows, columns] = weight[rows, here] - step_rate * expanded
        update_v[rows, columns] = expanded.astype(BF16)
        store(new_v, update_v, 1, i, rows, columns, here)
    for copy in copies:
        copy.wait()


def expand(*operands):
    depth = operands[3].shape[0]
    vmem = pl.BlockSpec(memory_space=pltpu.VMEM)
    hbm = pl.BlockSpec(memory_space=pltpu.HBM)
    return pl.pallas_call(
        expand_kernel,
        out_shape=(
            jax.ShapeDtypeStruct((depth, 1024), F32),
            jax.ShapeDtypeStruct((depth, 1024), BF16),
            jax.ShapeDtypeStruct((16, 256), F32),
            jax.ShapeDtypeStruct((16, 256), F32),
        ),
        in_specs=[vmem] * 7,
        out_specs=(hbm,) * 4,
        scratch_shapes=[
            pltpu.VMEM((depth, 512), F32),
            pltpu.VMEM((depth, 512), BF16),
            pltpu.SemaphoreType.DMA((2, 2, 2 * depth // ROW_TILE)),
            pltpu.SemaphoreType.DMA((2,)),
        ],
        compiler_params=pltpu.CompilerParams(vmem_limit_bytes=20 * 1024 * 1024),
    )(*operands)


def local(activations, out_grads, projector, weight, first_moment, second_moment):
    return tuple(
        expand(*reduce_and_gather(activations, out_grads, projector, weight, first_moment, second_moment))
    )


def solution(mesh):
    in_specs = (
        P("dp", "mp"),
        P("dp", None),
        P("mp", None),
        P("mp", None),
        P("dp", "mp"),
        P("dp", "mp"),
    )
    out_specs = (P("mp", None), P("mp", None), P("dp", "mp"), P("dp", "mp"))
    return jax.shard_map(local, mesh=mesh, in_specs=in_specs, out_specs=out_specs, check_vma=False)
```

```python
import functools

import jax
import jax.numpy as jnp
from jax import lax
from jax.experimental import pallas as pl
from jax.experimental.pallas import tpu as pltpu
from jax.sharding import PartitionSpec as P

first_decay = 0.9
second_decay = 0.999
first_bias = 1.0 - 0.9**2
second_bias = 1.0 - 0.999**2
epsilon = 1e-08
step_rate = 0.00025

MESH = pl.DeviceIdType.MESH
F32 = jnp.float32
BF16 = jnp.bfloat16
TOKEN_BLOCKS = 4
DEPTH_PARTS = 4
ROW_TILE = 512


WRAP_FIRST = ((False, False, True), (True, True, False))
HALVES = (1, 0)
PIECES = ((0, 1), (0, 0), (1, 1), (1, 0))


def place(wrap_first, v):
    return (v // 2, v % 2) if wrap_first else ((v + v // 2) % 2, v // 2)


MASKS = (7, 6, 5, 3, 4, 2, 1)


def bits(m):
    return m // 4, m // 2 % 2, m % 2


def reduce_kernel(
    acts,
    grads,
    proj,
    weight,
    first_moment,
    second_moment,
    other,
    own_new,
    own_update,
    proj_v,
    weight_v,
    first_new_ref,
    second_new_ref,
    gathered,
    own,
    acts_v,
    grads_v,
    mine,
    theirs,
    both,
    summed,
    parts,
    got1,
    sums,
    moments,
    states,
    seven,
    load_sem,
    pair_send,
    pair_recv,
    send_sem,
    recv_sem,
    fw_send,
    fw_recv,
):
    dp = lax.axis_index("dp")
    mp = lax.axis_index("mp")
    zh, c = mp // 2, mp % 2
    chip = (dp // 8, (dp // 2) % 4, zh * 2 + dp % 2)
    sibling = (dp, zh * 2 + 1 - c)

    terms = []
    for axis, v in enumerate(chip):
        options = (v, v + 1 - 2 * (v % 2), 3 - v)
        if axis == 2:
            terms.append([(o % 2, o // 2 * 2 + c) for o in options])
        else:
            terms.append([(o * (8, 2)[axis], 0) for o in options])

    def partner(half, flips, m):
        x, y, z = (
            terms[axis][(2 if WRAP_FIRST[half][axis] == (flips == 1) else 1) if bit else 0]
            for axis, bit in enumerate(bits(m))
        )
        return (x[0] + y[0] + z[0], z[1])

    def flip(at, m):
        return tuple(1 - v if bit else v for v, bit in zip(at, bits(m)))

    sets, members = [], []
    for half in range(2):
        places = [place(w, v) for w, v in zip(WRAP_FIRST[half], chip)]
        sets.append(tuple(p[0] for p in places))
        members.append(tuple(p[1] for p in places))

    depth = proj.shape[0] // DEPTH_PARTS
    load_parts = []

    def load_part(k):
        at = pl.ds(k * depth, depth)
        for n, (src, dst) in enumerate(((proj.at[at], proj_v.at[at]), (acts.at[:, at], acts_v.at[:, at]))):
            copy = pltpu.make_async_copy(src, dst, load_sem.at[2 * k + n])
            copy.start()
            load_parts.append(copy)

    load_part(0)
    barrier = pltpu.get_barrier_semaphore()
    for device in [sibling] + [partner(0, flips, m) for flips in (1, 2) for m in MASKS]:
        pl.semaphore_signal(barrier, inc=1, device_id=device, device_id_type=MESH)
    for k in range(1, DEPTH_PARTS):
        load_part(k)
    load_grads = []
    for half in range(2):
        for h in range(2):
            columns = pl.ds(pl.multiple_of(h * 512 + c * 256 + half * 128, 128), 128)
            copy = pltpu.make_async_copy(
                grads.at[:, columns],
                grads_v.at[half, :, pl.ds(h * 128, 128)],
                load_sem.at[2 * DEPTH_PARTS + 2 * half + h],
            )
            copy.start()
            load_grads.append(copy)
    load_moments = []
    for half in range(2):
        columns = pl.ds(half * 128, 128)
        for n, moment in enumerate((first_moment, second_moment)):
            copy = pltpu.make_async_copy(
                moment.at[:, columns],
                moments.at[(half, *members[half], n)],
                load_sem.at[4 + 2 * DEPTH_PARTS + 2 * half + n],
            )
            copy.start()
            load_moments.append(copy)
    load_weight = pltpu.make_async_copy(weight, weight_v, load_sem.at[8 + 2 * DEPTH_PARTS])

    started = []

    def send(src, dst, sent, arrived, device):
        copy = pltpu.make_async_remote_copy(
            src_ref=src, dst_ref=dst, send_sem=sent, recv_sem=arrived, device_id=device, device_id_type=MESH
        )
        copy.start()
        started.append(copy)
        return copy

    groups = []

    def spread(stage, piece, half, flips, source, target=None):
        at = (stage, piece, half)
        groups.append(at)
        for n, m in enumerate(MASKS):
            src = source(m)
            dst = src if target is None else target(n)
            pltpu.make_async_remote_copy(
                src_ref=src,
                dst_ref=dst,
                send_sem=send_sem.at[at],
                recv_sem=recv_sem.at[at],
                device_id=partner(half, flips, m),
                device_id_type=MESH,
            ).start()

    def arrived(stage, piece, half):
        pltpu.make_async_copy(seven, seven, recv_sem.at[stage, piece, half]).wait()

    for k in range(DEPTH_PARTS):
        at = pl.ds(k * depth, depth)
        load_parts[2 * k].wait()
        load_parts[2 * k + 1].wait()
        product = jnp.dot(acts_v[:, at], proj_v[at, :], preferred_element_type=F32)
        projected = product if k == 0 else projected + product
    block = projected.shape[0] // TOKEN_BLOCKS
    for t in range(TOKEN_BLOCKS):
        turned = projected[t * block : (t + 1) * block].T
        summed[t] = turned
        mine[t] = turned.astype(BF16)
    pl.semaphore_wait(barrier, 15)
    pair = [send(mine.at[t], theirs.at[t], pair_send.at[t], pair_recv.at[t], sibling) for t in range(TOKEN_BLOCKS)]
    for copy in load_grads:
        copy.wait()
    load_weight.start()
    for t in range(TOKEN_BLOCKS):
        pair[t].wait_recv()
        both[:, t * block : (t + 1) * block] = (summed[t] + theirs[t].astype(F32)).astype(BF16)

    def scatter(piece, half):
        spread(
            1,
            piece,
            half,
            1,
            lambda m: parts.at[(half, *flip(sets[half], m), piece)],
            lambda n: got1.at[half, piece, n],
        )

    for half in HALVES:
        product = jnp.dot(both[...], grads_v[half], preferred_element_type=F32).astype(BF16)
        for x in range(4):
            for y in range(4):
                for z in range(4):
                    row, column = x * 128 + y * 32 + z % 2 * 16, z // 2 * 128
                    at = [place(w, v) for w, v in zip(WRAP_FIRST[half], (x, y, z))]
                    index = tuple(p[0] for p in at) + tuple(p[1] for p in at)
                    parts[(half, *index)] = product[row : row + 16, column : column + 128]
        scatter(0, half)
    for half in HALVES:
        scatter(1, half)

    for copy in load_moments:
        copy.wait()
    for half in HALVES:
        spread(0, 0, half, 2, lambda m: moments.at[(half, *members[half])])

    for piece, half in PIECES:
        arrived(1, piece, half)
        total = parts[(half, *sets[half], piece)].astype(F32)
        for n in range(7):
            total += got1[half, piece, n].astype(F32)
        here = (half, *members[half], piece)
        sums[here] = total.astype(BF16)
        spread(2, piece, half, 2, lambda m: sums.at[here])

    for half in HALVES:
        arrived(0, 0, half)
    for piece, half in PIECES:
        arrived(2, piece, half)
        for j in range(2):
            for k in range(2):
                coefficients = sums[half, 0, 0, 0, piece, j, k].astype(F32)
                for n in range(1, 8):
                    coefficients += sums[(half, *bits(n), piece, j, k)].astype(F32)
                first_new = first_decay * moments[half, piece, j, k, 0] + (1.0 - first_decay) * coefficients
                second_new = (
                    second_decay * moments[half, piece, j, k, 1]
                    + (1.0 - second_decay) * coefficients * coefficients
                )
                normalized = first_new / first_bias / (jnp.sqrt(second_new / second_bias) + epsilon)
                gathered[(c, half, *sets[half], piece, j, k)] = normalized.astype(BF16)
                states[half, piece, j, k, 0] = first_new
                states[half, piece, j, k, 1] = second_new
        spread(3, piece, half, 1, lambda m: gathered.at[(c, half, *sets[half], piece)])
    for half in range(2):
        columns = slice(half * 128, (half + 1) * 128)
        first_new_ref[:, columns] = states[(half, *members[half], 0)]
        second_new_ref[:, columns] = states[(half, *members[half], 1)]

    forwards = []
    for piece, half in PIECES:
        arrived(3, piece, half)
        block = gathered.at[c, half, :, :, :, piece]
        forwards.append(send(block, block, fw_send.at[piece, half], fw_recv.at[piece, half], sibling))

    def order(core, half, target):
        for x in range(4):
            for y in range(4):
                for z in range(4):
                    row, column = x * 128 + y * 32 + z % 2 * 16, z // 2 * 256 + half * 128
                    at = [place(w, v) for w, v in zip(WRAP_FIRST[half], (x, y, z))]
                    index = tuple(p[0] for p in at) + tuple(p[1] for p in at)
                    target[row : row + 16, column : column + 128] = gathered[(core, half, *index)]

    for half in HALVES:
        order(c, half, own)
    load_weight.wait()
    for rows, columns, here in column_tiles(weight_v.shape[0], c):
        expanded = jnp.dot(proj_v[rows, :], own[:, columns], preferred_element_type=F32)
        own_new[rows, columns] = weight_v[rows, here] - step_rate * expanded
        own_update[rows, columns] = expanded.astype(BF16)

    for at in groups:
        pltpu.make_async_copy(seven, seven, send_sem.at[at]).wait()
    for copy in started:
        copy.wait_send()
    for copy in forwards:
        copy.wait_recv()
    for half in HALVES:
        order(1 - c, half, other)


def column_tiles(depth, core):
    for h in range(2):
        for i in range(depth // ROW_TILE):
            rows = pl.ds(i * ROW_TILE, ROW_TILE)
            yield rows, pl.ds(h * 256, 256), pl.ds(pl.multiple_of(h * 512 + core * 256, 256), 256)


def reduce_and_gather(*operands):
    proj, weight = operands[2], operands[3]
    vmem = pl.BlockSpec(memory_space=pltpu.VMEM)
    hbm = pl.BlockSpec(memory_space=pltpu.HBM)
    dma = pltpu.SemaphoreType.DMA
    return pl.pallas_call(
        reduce_kernel,
        out_shape=(
            pltpu.VMEM((512, 512), BF16),
            pltpu.VMEM((proj.shape[0], 512), F32),
            pltpu.VMEM((proj.shape[0], 512), BF16),
            pltpu.VMEM(proj.shape, BF16),
            pltpu.VMEM(weight.shape, F32),
            pltpu.VMEM((16, 256), F32),
            pltpu.VMEM((16, 256), F32),
        ),
        in_specs=[hbm] * 6,
        out_specs=(vmem,) * 7,
        scratch_shapes=[
            pltpu.VMEM((2, 2, 2, 2, 2, 2, 2, 2, 16, 128), BF16),
            pltpu.VMEM((512, 512), BF16),
            pltpu.VMEM((512, 2048), BF16),
            pltpu.VMEM((2, 512, 256), BF16),
            pltpu.VMEM((TOKEN_BLOCKS, 512, 512 // TOKEN_BLOCKS), BF16),
            pltpu.VMEM((TOKEN_BLOCKS, 512, 512 // TOKEN_BLOCKS), BF16),
            pltpu.VMEM((512, 512), BF16),
            pltpu.VMEM((TOKEN_BLOCKS, 512, 512 // TOKEN_BLOCKS), F32),
            pltpu.VMEM((2, 2, 2, 2, 2, 2, 2, 16, 128), BF16),
            pltpu.VMEM((2, 2, 7, 2, 2, 16, 128), BF16),
            pltpu.VMEM((2, 2, 2, 2, 2, 2, 2, 16, 128), BF16),
            pltpu.VMEM((2, 2, 2, 2, 2, 16, 128), F32),
            pltpu.VMEM((2, 2, 2, 2, 2, 16, 128), F32),
            pltpu.VMEM((7, 2, 2, 16, 128), BF16),
            dma((9 + 2 * DEPTH_PARTS,)),
            dma((TOKEN_BLOCKS,)),
            dma((TOKEN_BLOCKS,)),
            dma((4, 2, 2)),
            dma((4, 2, 2)),
            dma((2, 2)),
            dma((2, 2)),
        ],
        compiler_params=pltpu.CompilerParams(
            collective_id=0, has_side_effects=True, vmem_limit_bytes=24 * 1024 * 1024
        ),
    )(*(pltpu.with_memory_space_constraint(a, pltpu.HBM) for a in operands))


def expand_kernel(
    other,
    own_new,
    own_update,
    proj,
    weight,
    first_in,
    second_in,
    new_weight,
    update,
    first_out,
    second_out,
    new_v,
    update_v,
    sems,
    state_sems,
):
    c = lax.axis_index("mp") % 2
    copies = [
        pltpu.make_async_copy(first_in, first_out, state_sems.at[0]),
        pltpu.make_async_copy(second_in, second_out, state_sems.at[1]),
    ]
    for copy in copies:
        copy.start()

    def store(new, upd, core, i, rows, columns, here):
        for n, (src, dst) in enumerate(((new, new_weight), (upd, update))):
            copy = pltpu.make_async_copy(src.at[rows, columns], dst.at[rows, here], sems.at[core, n, i])
            copy.start()
            copies.append(copy)

    depth = weight.shape[0]
    for i, at in enumerate(column_tiles(depth, c)):
        store(own_new, own_update, 0, i, *at)
    for i, (rows, columns, here) in enumerate(column_tiles(depth, 1 - c)):
        expanded = jnp.dot(proj[rows, :], other[:, columns], preferred_element_type=F32)
        new_v[rows, columns] = weight[rows, here] - step_rate * expanded
        update_v[rows, columns] = expanded.astype(BF16)
        store(new_v, update_v, 1, i, rows, columns, here)
    for copy in copies:
        copy.wait()


def expand(*operands):
    depth = operands[3].shape[0]
    vmem = pl.BlockSpec(memory_space=pltpu.VMEM)
    hbm = pl.BlockSpec(memory_space=pltpu.HBM)
    return pl.pallas_call(
        expand_kernel,
        out_shape=(
            jax.ShapeDtypeStruct((depth, 1024), F32),
            jax.ShapeDtypeStruct((depth, 1024), BF16),
            jax.ShapeDtypeStruct((16, 256), F32),
            jax.ShapeDtypeStruct((16, 256), F32),
        ),
        in_specs=[vmem] * 7,
        out_specs=(hbm,) * 4,
        scratch_shapes=[
            pltpu.VMEM((depth, 512), F32),
            pltpu.VMEM((depth, 512), BF16),
            pltpu.SemaphoreType.DMA((2, 2, 2 * depth // ROW_TILE)),
            pltpu.SemaphoreType.DMA((2,)),
        ],
        compiler_params=pltpu.CompilerParams(vmem_limit_bytes=20 * 1024 * 1024),
    )(*operands)


def local(activations, out_grads, projector, weight, first_moment, second_moment):
    return tuple(
        expand(*reduce_and_gather(activations, out_grads, projector, weight, first_moment, second_moment))
    )


def solution(mesh):
    in_specs = (
        P("dp", "mp"),
        P("dp", None),
        P("mp", None),
        P("mp", None),
        P("dp", "mp"),
        P("dp", "mp"),
    )
    out_specs = (P("mp", None), P("mp", None), P("dp", "mp"), P("dp", "mp"))
    return jax.shard_map(local, mesh=mesh, in_specs=in_specs, out_specs=out_specs, check_vma=False)
```

```python
import functools

import jax
import jax.numpy as jnp
from jax import lax
from jax.experimental import pallas as pl
from jax.experimental.pallas import tpu as pltpu
from jax.sharding import PartitionSpec as P

first_decay = 0.9
second_decay = 0.999
first_bias = 1.0 - 0.9**2
second_bias = 1.0 - 0.999**2
epsilon = 1e-08
step_rate = 0.00025

MESH = pl.DeviceIdType.MESH
F32 = jnp.float32
BF16 = jnp.bfloat16
TOKEN_BLOCKS = 4
DEPTHS = (768, 512, 512, 256)
EARLY_TILES = 2
ROW_TILE = 512


WRAP_FIRST = ((False, False, True), (True, True, False))
HALVES = (1, 0)
PIECES = ((0, 1), (0, 0), (1, 1), (1, 0))


def place(wrap_first, v):
    return (v // 2, v % 2) if wrap_first else ((v + v // 2) % 2, v // 2)


MASKS = (7, 6, 5, 3, 4, 2, 1)


def bits(m):
    return m // 4, m // 2 % 2, m % 2


def reduce_kernel(
    acts,
    grads,
    proj,
    weight,
    first_moment,
    second_moment,
    own,
    other,
    own_new,
    own_update,
    proj_v,
    weight_v,
    first_new_ref,
    second_new_ref,
    gathered,
    acts_v,
    grads_v,
    mine,
    theirs,
    both,
    summed,
    parts,
    got1,
    sums,
    moments,
    states,
    seven,
    load_sem,
    pair_send,
    pair_recv,
    send_sem,
    recv_sem,
    fw_send,
    fw_recv,
):
    dp = lax.axis_index("dp")
    mp = lax.axis_index("mp")
    zh, c = mp // 2, mp % 2
    chip = (dp // 8, (dp // 2) % 4, zh * 2 + dp % 2)
    sibling = (dp, zh * 2 + 1 - c)

    terms = []
    for axis, v in enumerate(chip):
        options = (v, v + 1 - 2 * (v % 2), 3 - v)
        if axis == 2:
            terms.append([(o % 2, o // 2 * 2 + c) for o in options])
        else:
            terms.append([(o * (8, 2)[axis], 0) for o in options])

    def partner(half, flips, m):
        x, y, z = (
            terms[axis][(2 if WRAP_FIRST[half][axis] == (flips == 1) else 1) if bit else 0]
            for axis, bit in enumerate(bits(m))
        )
        return (x[0] + y[0] + z[0], z[1])

    def flip(at, m):
        return tuple(1 - v if bit else v for v, bit in zip(at, bits(m)))

    sets, members = [], []
    for half in range(2):
        places = [place(w, v) for w, v in zip(WRAP_FIRST[half], chip)]
        sets.append(tuple(p[0] for p in places))
        members.append(tuple(p[1] for p in places))

    load_parts = []

    def depth_part(k):
        return pl.ds(sum(DEPTHS[:k]), DEPTHS[k])

    def load_part(k):
        at = depth_part(k)
        for n, (src, dst) in enumerate(((proj.at[at], proj_v.at[at]), (acts.at[:, at], acts_v.at[:, at]))):
            copy = pltpu.make_async_copy(src, dst, load_sem.at[2 * k + n])
            copy.start()
            load_parts.append(copy)

    load_part(0)
    barrier = pltpu.get_barrier_semaphore()
    for device in [sibling] + [partner(0, flips, m) for flips in (1, 2) for m in MASKS]:
        pl.semaphore_signal(barrier, inc=1, device_id=device, device_id_type=MESH)
    for k in range(1, len(DEPTHS)):
        load_part(k)
    load_grads = []
    for half in range(2):
        for h in range(2):
            columns = pl.ds(pl.multiple_of(h * 512 + c * 256 + half * 128, 128), 128)
            copy = pltpu.make_async_copy(
                grads.at[:, columns],
                grads_v.at[half, :, pl.ds(h * 128, 128)],
                load_sem.at[2 * len(DEPTHS) + 2 * half + h],
            )
            copy.start()
            load_grads.append(copy)
    load_moments = []
    for half in range(2):
        columns = pl.ds(half * 128, 128)
        for n, moment in enumerate((first_moment, second_moment)):
            copy = pltpu.make_async_copy(
                moment.at[:, columns],
                moments.at[(half, *members[half], n)],
                load_sem.at[4 + 2 * len(DEPTHS) + 2 * half + n],
            )
            copy.start()
            load_moments.append(copy)
    load_weight = pltpu.make_async_copy(weight, weight_v, load_sem.at[8 + 2 * len(DEPTHS)])

    started = []

    def send(src, dst, sent, arrived, device):
        copy = pltpu.make_async_remote_copy(
            src_ref=src, dst_ref=dst, send_sem=sent, recv_sem=arrived, device_id=device, device_id_type=MESH
        )
        copy.start()
        started.append(copy)
        return copy

    groups = []

    def spread(stage, piece, half, flips, source, target=None):
        at = (stage, piece, half)
        groups.append(at)
        for n, m in enumerate(MASKS):
            src = source(m)
            dst = src if target is None else target(n)
            pltpu.make_async_remote_copy(
                src_ref=src,
                dst_ref=dst,
                send_sem=send_sem.at[at],
                recv_sem=recv_sem.at[at],
                device_id=partner(half, flips, m),
                device_id_type=MESH,
            ).start()

    def arrived(stage, piece, half):
        pltpu.make_async_copy(seven, seven, recv_sem.at[stage, piece, half]).wait()

    for k in range(len(DEPTHS)):
        at = depth_part(k)
        load_parts[2 * k].wait()
        load_parts[2 * k + 1].wait()
        product = jnp.dot(acts_v[:, at], proj_v[at, :], preferred_element_type=F32)
        projected = product if k == 0 else projected + product
    block = projected.shape[0] // TOKEN_BLOCKS
    for t in range(TOKEN_BLOCKS):
        turned = projected[t * block : (t + 1) * block].T
        summed[t] = turned
        mine[t] = turned.astype(BF16)
    pl.semaphore_wait(barrier, 15)
    pair = [send(mine.at[t], theirs.at[t], pair_send.at[t], pair_recv.at[t], sibling) for t in range(TOKEN_BLOCKS)]
    for copy in load_grads:
        copy.wait()
    load_weight.start()
    for t in range(TOKEN_BLOCKS):
        pair[t].wait_recv()
        both[:, t * block : (t + 1) * block] = (summed[t] + theirs[t].astype(F32)).astype(BF16)

    def scatter(piece, half):
        spread(
            1,
            piece,
            half,
            1,
            lambda m: parts.at[(half, *flip(sets[half], m), piece)],
            lambda n: got1.at[half, piece, n],
        )

    for piece, half in PIECES:
        blocks = [x for x in range(4) if place(WRAP_FIRST[half][0], x)[1] == piece]
        left = jnp.concatenate([both[x * 128 : (x + 1) * 128, :] for x in blocks], axis=0)
        product = jnp.dot(left, grads_v[half], preferred_element_type=F32).astype(BF16)
        for i, x in enumerate(blocks):
            for y in range(4):
                for z in range(4):
                    row, column = i * 128 + y * 32 + z % 2 * 16, z // 2 * 128
                    at = [place(w, v) for w, v in zip(WRAP_FIRST[half], (x, y, z))]
                    index = tuple(p[0] for p in at) + tuple(p[1] for p in at)
                    parts[(half, *index)] = product[row : row + 16, column : column + 128]
        scatter(piece, half)

    for copy in load_moments:
        copy.wait()
    for half in HALVES:
        spread(0, 0, half, 2, lambda m: moments.at[(half, *members[half])])

    for piece, half in PIECES:
        arrived(1, piece, half)
        total = parts[(half, *sets[half], piece)].astype(F32)
        for n in range(7):
            total += got1[half, piece, n].astype(F32)
        here = (half, *members[half], piece)
        sums[here] = total.astype(BF16)
        spread(2, piece, half, 2, lambda m: sums.at[here])

    for half in HALVES:
        arrived(0, 0, half)
    for piece, half in PIECES:
        arrived(2, piece, half)
        for j in range(2):
            for k in range(2):
                coefficients = sums[half, 0, 0, 0, piece, j, k].astype(F32)
                for n in range(1, 8):
                    coefficients += sums[(half, *bits(n), piece, j, k)].astype(F32)
                first_new = first_decay * moments[half, piece, j, k, 0] + (1.0 - first_decay) * coefficients
                second_new = (
                    second_decay * moments[half, piece, j, k, 1]
                    + (1.0 - second_decay) * coefficients * coefficients
                )
                normalized = first_new / first_bias / (jnp.sqrt(second_new / second_bias) + epsilon)
                gathered[(c, half, *sets[half], piece, j, k)] = normalized.astype(BF16)
                states[half, piece, j, k, 0] = first_new
                states[half, piece, j, k, 1] = second_new
        spread(3, piece, half, 1, lambda m: gathered.at[(c, half, *sets[half], piece)])
    for half in range(2):
        columns = slice(half * 128, (half + 1) * 128)
        first_new_ref[:, columns] = states[(half, *members[half], 0)]
        second_new_ref[:, columns] = states[(half, *members[half], 1)]

    forwards = []
    for piece, half in PIECES:
        arrived(3, piece, half)
        block = gathered.at[c, half, :, :, :, piece]
        forwards.append(send(block, block, fw_send.at[piece, half], fw_recv.at[piece, half], sibling))

    def order(core, half, target):
        for x in range(4):
            for y in range(4):
                for z in range(4):
                    row, column = x * 128 + y * 32 + z % 2 * 16, z // 2 * 256 + half * 128
                    at = [place(w, v) for w, v in zip(WRAP_FIRST[half], (x, y, z))]
                    index = tuple(p[0] for p in at) + tuple(p[1] for p in at)
                    target[row : row + 16, column : column + 128] = gathered[(core, half, *index)]

    for half in HALVES:
        order(c, half, own)
    load_weight.wait()
    for i, (rows, columns, here) in enumerate(column_tiles(weight_v.shape[0], c)):
        if i < EARLY_TILES:
            expanded = jnp.dot(proj_v[rows, :], own[:, columns], preferred_element_type=F32)
            own_new[i] = weight_v[rows, here] - step_rate * expanded
            own_update[i] = expanded.astype(BF16)

    for at in groups:
        pltpu.make_async_copy(seven, seven, send_sem.at[at]).wait()
    for copy in started:
        copy.wait_send()
    for copy in forwards:
        copy.wait_recv()
    for half in HALVES:
        order(1 - c, half, other)


def column_tiles(depth, core):
    for h in range(2):
        for i in range(depth // ROW_TILE):
            rows = pl.ds(i * ROW_TILE, ROW_TILE)
            yield rows, pl.ds(h * 256, 256), pl.ds(pl.multiple_of(h * 512 + core * 256, 256), 256)


def reduce_and_gather(*operands):
    proj, weight = operands[2], operands[3]
    vmem = pl.BlockSpec(memory_space=pltpu.VMEM)
    hbm = pl.BlockSpec(memory_space=pltpu.HBM)
    dma = pltpu.SemaphoreType.DMA
    return pl.pallas_call(
        reduce_kernel,
        out_shape=(
            pltpu.VMEM((512, 512), BF16),
            pltpu.VMEM((512, 512), BF16),
            pltpu.VMEM((EARLY_TILES, ROW_TILE, 256), F32),
            pltpu.VMEM((EARLY_TILES, ROW_TILE, 256), BF16),
            pltpu.VMEM(proj.shape, BF16),
            pltpu.VMEM(weight.shape, F32),
            pltpu.VMEM((16, 256), F32),
            pltpu.VMEM((16, 256), F32),
        ),
        in_specs=[hbm] * 6,
        out_specs=(vmem,) * 8,
        scratch_shapes=[
            pltpu.VMEM((2, 2, 2, 2, 2, 2, 2, 2, 16, 128), BF16),
            pltpu.VMEM((512, 2048), BF16),
            pltpu.VMEM((2, 512, 256), BF16),
            pltpu.VMEM((TOKEN_BLOCKS, 512, 512 // TOKEN_BLOCKS), BF16),
            pltpu.VMEM((TOKEN_BLOCKS, 512, 512 // TOKEN_BLOCKS), BF16),
            pltpu.VMEM((512, 512), BF16),
            pltpu.VMEM((TOKEN_BLOCKS, 512, 512 // TOKEN_BLOCKS), F32),
            pltpu.VMEM((2, 2, 2, 2, 2, 2, 2, 16, 128), BF16),
            pltpu.VMEM((2, 2, 7, 2, 2, 16, 128), BF16),
            pltpu.VMEM((2, 2, 2, 2, 2, 2, 2, 16, 128), BF16),
            pltpu.VMEM((2, 2, 2, 2, 2, 16, 128), F32),
            pltpu.VMEM((2, 2, 2, 2, 2, 16, 128), F32),
            pltpu.VMEM((7, 2, 2, 16, 128), BF16),
            dma((9 + 2 * len(DEPTHS),)),
            dma((TOKEN_BLOCKS,)),
            dma((TOKEN_BLOCKS,)),
            dma((4, 2, 2)),
            dma((4, 2, 2)),
            dma((2, 2)),
            dma((2, 2)),
        ],
        compiler_params=pltpu.CompilerParams(
            collective_id=0, has_side_effects=True, vmem_limit_bytes=24 * 1024 * 1024
        ),
    )(*(pltpu.with_memory_space_constraint(a, pltpu.HBM) for a in operands))


def expand_kernel(
    own,
    other,
    own_new,
    own_update,
    proj,
    weight,
    first_in,
    second_in,
    new_weight,
    update,
    first_out,
    second_out,
    new_v,
    update_v,
    sems,
    state_sems,
):
    c = lax.axis_index("mp") % 2
    copies = [
        pltpu.make_async_copy(first_in, first_out, state_sems.at[0]),
        pltpu.make_async_copy(second_in, second_out, state_sems.at[1]),
    ]
    for copy in copies:
        copy.start()

    def store(new, upd, core, i, rows, here):
        for n, (src, dst) in enumerate(((new, new_weight), (upd, update))):
            copy = pltpu.make_async_copy(src.at[i], dst.at[rows, here], sems.at[core, n, i])
            copy.start()
            copies.append(copy)

    depth = weight.shape[0]
    for core, normalized in ((0, own), (1, other)):
        for i, (rows, columns, here) in enumerate(column_tiles(depth, c if core == 0 else 1 - c)):
            if core == 0 and i < EARLY_TILES:
                store(own_new, own_update, core, i, rows, here)
                continue
            expanded = jnp.dot(proj[rows, :], normalized[:, columns], preferred_element_type=F32)
            new_v[core, i] = weight[rows, here] - step_rate * expanded
            update_v[core, i] = expanded.astype(BF16)
            store(new_v.at[core], update_v.at[core], core, i, rows, here)
    for copy in copies:
        copy.wait()


def expand(*operands):
    depth = operands[4].shape[0]
    tiles = 2 * depth // ROW_TILE
    vmem = pl.BlockSpec(memory_space=pltpu.VMEM)
    hbm = pl.BlockSpec(memory_space=pltpu.HBM)
    return pl.pallas_call(
        expand_kernel,
        out_shape=(
            jax.ShapeDtypeStruct((depth, 1024), F32),
            jax.ShapeDtypeStruct((depth, 1024), BF16),
            jax.ShapeDtypeStruct((16, 256), F32),
            jax.ShapeDtypeStruct((16, 256), F32),
        ),
        in_specs=[vmem] * 8,
        out_specs=(hbm,) * 4,
        scratch_shapes=[
            pltpu.VMEM((2, tiles, ROW_TILE, 256), F32),
            pltpu.VMEM((2, tiles, ROW_TILE, 256), BF16),
            pltpu.SemaphoreType.DMA((2, 2, tiles)),
            pltpu.SemaphoreType.DMA((2,)),
        ],
        compiler_params=pltpu.CompilerParams(vmem_limit_bytes=20 * 1024 * 1024),
    )(*operands)


def local(activations, out_grads, projector, weight, first_moment, second_moment):
    return tuple(
        expand(*reduce_and_gather(activations, out_grads, projector, weight, first_moment, second_moment))
    )


def solution(mesh):
    in_specs = (
        P("dp", "mp"),
        P("dp", None),
        P("mp", None),
        P("mp", None),
        P("dp", "mp"),
        P("dp", "mp"),
    )
    out_specs = (P("mp", None), P("mp", None), P("dp", "mp"), P("dp", "mp"))
    return jax.shard_map(local, mesh=mesh, in_specs=in_specs, out_specs=out_specs, check_vma=False)
```

```python
import functools

import jax
import jax.numpy as jnp
from jax import lax
from jax.experimental import pallas as pl
from jax.experimental.pallas import tpu as pltpu
from jax.sharding import PartitionSpec as P

first_decay = 0.9
second_decay = 0.999
first_bias = 1.0 - 0.9**2
second_bias = 1.0 - 0.999**2
epsilon = 1e-08
step_rate = 0.00025

MESH = pl.DeviceIdType.MESH
F32 = jnp.float32
BF16 = jnp.bfloat16
TOKEN_BLOCKS = 4
DEPTHS = (768, 512, 512, 256)
EARLY_TILES = 2
ROW_TILE = 512


WRAP_FIRST = ((False, False, True), (True, True, False))
HALVES = (1, 0)
PIECES = ((0, 1), (0, 0), (1, 1), (1, 0))
ARRIVING = ((0, 0), (0, 1), (1, 0), (1, 1))


def place(wrap_first, v):
    return (v // 2, v % 2) if wrap_first else ((v + v // 2) % 2, v // 2)


MASKS = (7, 6, 5, 3, 4, 2, 1)


def bits(m):
    return m // 4, m // 2 % 2, m % 2


def reduce_kernel(
    acts,
    grads,
    proj,
    weight,
    first_moment,
    second_moment,
    own,
    other,
    own_new,
    own_update,
    proj_v,
    weight_v,
    first_new_ref,
    second_new_ref,
    gathered,
    acts_v,
    grads_v,
    mine,
    theirs,
    both,
    summed,
    parts,
    got1,
    sums,
    moments,
    states,
    seven,
    load_sem,
    pair_send,
    pair_recv,
    send_sem,
    recv_sem,
    fw_send,
    fw_recv,
):
    dp = lax.axis_index("dp")
    mp = lax.axis_index("mp")
    zh, c = mp // 2, mp % 2
    chip = (dp // 8, (dp // 2) % 4, zh * 2 + dp % 2)
    sibling = (dp, zh * 2 + 1 - c)

    terms = []
    for axis, v in enumerate(chip):
        options = (v, v + 1 - 2 * (v % 2), 3 - v)
        if axis == 2:
            terms.append([(o % 2, o // 2 * 2 + c) for o in options])
        else:
            terms.append([(o * (8, 2)[axis], 0) for o in options])

    def partner(half, flips, m):
        x, y, z = (
            terms[axis][(2 if WRAP_FIRST[half][axis] == (flips == 1) else 1) if bit else 0]
            for axis, bit in enumerate(bits(m))
        )
        return (x[0] + y[0] + z[0], z[1])

    def flip(at, m):
        return tuple(1 - v if bit else v for v, bit in zip(at, bits(m)))

    sets, members = [], []
    for half in range(2):
        places = [place(w, v) for w, v in zip(WRAP_FIRST[half], chip)]
        sets.append(tuple(p[0] for p in places))
        members.append(tuple(p[1] for p in places))

    load_parts = []

    def depth_part(k):
        return pl.ds(sum(DEPTHS[:k]), DEPTHS[k])

    def load_part(k):
        at = depth_part(k)
        for n, (src, dst) in enumerate(((proj.at[at], proj_v.at[at]), (acts.at[:, at], acts_v.at[:, at]))):
            copy = pltpu.make_async_copy(src, dst, load_sem.at[2 * k + n])
            copy.start()
            load_parts.append(copy)

    load_part(0)
    barrier = pltpu.get_barrier_semaphore()
    for device in [sibling] + [partner(0, flips, m) for flips in (1, 2) for m in MASKS]:
        pl.semaphore_signal(barrier, inc=1, device_id=device, device_id_type=MESH)
    for k in range(1, len(DEPTHS)):
        load_part(k)
    load_grads = []
    for half in range(2):
        for h in range(2):
            columns = pl.ds(pl.multiple_of(h * 512 + c * 256 + half * 128, 128), 128)
            copy = pltpu.make_async_copy(
                grads.at[:, columns],
                grads_v.at[half, :, pl.ds(h * 128, 128)],
                load_sem.at[2 * len(DEPTHS) + 2 * half + h],
            )
            copy.start()
            load_grads.append(copy)
    load_moments = []
    for half in range(2):
        columns = pl.ds(half * 128, 128)
        for n, moment in enumerate((first_moment, second_moment)):
            copy = pltpu.make_async_copy(
                moment.at[:, columns],
                moments.at[(half, *members[half], n)],
                load_sem.at[4 + 2 * len(DEPTHS) + 2 * half + n],
            )
            copy.start()
            load_moments.append(copy)
    load_weight = pltpu.make_async_copy(weight, weight_v, load_sem.at[8 + 2 * len(DEPTHS)])

    started = []

    def send(src, dst, sent, arrived, device):
        copy = pltpu.make_async_remote_copy(
            src_ref=src, dst_ref=dst, send_sem=sent, recv_sem=arrived, device_id=device, device_id_type=MESH
        )
        copy.start()
        started.append(copy)
        return copy

    groups = []

    def spread(stage, piece, half, flips, source, target=None):
        at = (stage, piece, half)
        groups.append(at)
        for n, m in enumerate(MASKS):
            src = source(m)
            dst = src if target is None else target(n)
            pltpu.make_async_remote_copy(
                src_ref=src,
                dst_ref=dst,
                send_sem=send_sem.at[at],
                recv_sem=recv_sem.at[at],
                device_id=partner(half, flips, m),
                device_id_type=MESH,
            ).start()

    def arrived(stage, piece, half):
        pltpu.make_async_copy(seven, seven, recv_sem.at[stage, piece, half]).wait()

    for k in range(len(DEPTHS)):
        at = depth_part(k)
        load_parts[2 * k].wait()
        load_parts[2 * k + 1].wait()
        product = jnp.dot(acts_v[:, at], proj_v[at, :], preferred_element_type=F32)
        projected = product if k == 0 else projected + product
    block = projected.shape[0] // TOKEN_BLOCKS
    pair = []
    for t in range(TOKEN_BLOCKS):
        turned = projected[t * block : (t + 1) * block].T
        summed[t] = turned
        mine[t] = turned.astype(BF16)
        if t == 0:
            pl.semaphore_wait(barrier, 15)
        pair.append(send(mine.at[t], theirs.at[t], pair_send.at[t], pair_recv.at[t], sibling))
    for copy in load_grads:
        copy.wait()
    load_weight.start()
    for t in range(TOKEN_BLOCKS):
        pair[t].wait_recv()
        both[:, t * block : (t + 1) * block] = (summed[t] + theirs[t].astype(F32)).astype(BF16)

    def scatter(piece, half):
        spread(
            1,
            piece,
            half,
            1,
            lambda m: parts.at[(half, *flip(sets[half], m), piece)],
            lambda n: got1.at[half, piece, n],
        )

    for piece, half in PIECES:
        blocks = [x for x in range(4) if place(WRAP_FIRST[half][0], x)[1] == piece]
        left = jnp.concatenate([both[x * 128 : (x + 1) * 128, :] for x in blocks], axis=0)
        product = jnp.dot(left, grads_v[half], preferred_element_type=F32).astype(BF16)
        for i, x in enumerate(blocks):
            for y in range(4):
                for z in range(4):
                    row, column = i * 128 + y * 32 + z % 2 * 16, z // 2 * 128
                    at = [place(w, v) for w, v in zip(WRAP_FIRST[half], (x, y, z))]
                    index = tuple(p[0] for p in at) + tuple(p[1] for p in at)
                    parts[(half, *index)] = product[row : row + 16, column : column + 128]
        scatter(piece, half)

    for copy in load_moments:
        copy.wait()
    for half in HALVES:
        spread(0, 0, half, 2, lambda m: moments.at[(half, *members[half])])

    for piece, half in ARRIVING:
        arrived(1, piece, half)
        total = parts[(half, *sets[half], piece)].astype(F32)
        for n in range(7):
            total += got1[half, piece, n].astype(F32)
        here = (half, *members[half], piece)
        sums[here] = total.astype(BF16)
        spread(2, piece, half, 2, lambda m: sums.at[here])

    for half in HALVES:
        arrived(0, 0, half)
    for piece, half in PIECES:
        arrived(2, piece, half)
        for j in range(2):
            for k in range(2):
                coefficients = sums[half, 0, 0, 0, piece, j, k].astype(F32)
                for n in range(1, 8):
                    coefficients += sums[(half, *bits(n), piece, j, k)].astype(F32)
                first_new = first_decay * moments[half, piece, j, k, 0] + (1.0 - first_decay) * coefficients
                second_new = (
                    second_decay * moments[half, piece, j, k, 1]
                    + (1.0 - second_decay) * coefficients * coefficients
                )
                normalized = first_new / first_bias / (jnp.sqrt(second_new / second_bias) + epsilon)
                gathered[(c, half, *sets[half], piece, j, k)] = normalized.astype(BF16)
                states[half, piece, j, k, 0] = first_new
                states[half, piece, j, k, 1] = second_new
        spread(3, piece, half, 1, lambda m: gathered.at[(c, half, *sets[half], piece)])
    for half in range(2):
        columns = slice(half * 128, (half + 1) * 128)
        first_new_ref[:, columns] = states[(half, *members[half], 0)]
        second_new_ref[:, columns] = states[(half, *members[half], 1)]

    forwards = []
    for piece, half in ARRIVING:
        arrived(3, piece, half)
        block = gathered.at[c, half, :, :, :, piece]
        forwards.append(send(block, block, fw_send.at[piece, half], fw_recv.at[piece, half], sibling))

    def order(core, half, target):
        for x in range(4):
            for y in range(4):
                for z in range(4):
                    row, column = x * 128 + y * 32 + z % 2 * 16, z // 2 * 256 + half * 128
                    at = [place(w, v) for w, v in zip(WRAP_FIRST[half], (x, y, z))]
                    index = tuple(p[0] for p in at) + tuple(p[1] for p in at)
                    target[row : row + 16, column : column + 128] = gathered[(core, half, *index)]

    for half in HALVES:
        order(c, half, own)
    load_weight.wait()
    for i, (rows, columns, here) in enumerate(column_tiles(weight_v.shape[0], c)):
        if i < EARLY_TILES:
            expanded = jnp.dot(proj_v[rows, :], own[:, columns], preferred_element_type=F32)
            own_new[i] = weight_v[rows, here] - step_rate * expanded
            own_update[i] = expanded.astype(BF16)

    for at in groups:
        pltpu.make_async_copy(seven, seven, send_sem.at[at]).wait()
    for copy in started:
        copy.wait_send()
    for copy in forwards:
        copy.wait_recv()
    for half in HALVES:
        order(1 - c, half, other)


def column_tiles(depth, core):
    for h in range(2):
        for i in range(depth // ROW_TILE):
            rows = pl.ds(i * ROW_TILE, ROW_TILE)
            yield rows, pl.ds(h * 256, 256), pl.ds(pl.multiple_of(h * 512 + core * 256, 256), 256)


def reduce_and_gather(*operands):
    proj, weight = operands[2], operands[3]
    vmem = pl.BlockSpec(memory_space=pltpu.VMEM)
    hbm = pl.BlockSpec(memory_space=pltpu.HBM)
    dma = pltpu.SemaphoreType.DMA
    return pl.pallas_call(
        reduce_kernel,
        out_shape=(
            pltpu.VMEM((512, 512), BF16),
            pltpu.VMEM((512, 512), BF16),
            pltpu.VMEM((EARLY_TILES, ROW_TILE, 256), F32),
            pltpu.VMEM((EARLY_TILES, ROW_TILE, 256), BF16),
            pltpu.VMEM(proj.shape, BF16),
            pltpu.VMEM(weight.shape, F32),
            pltpu.VMEM((16, 256), F32),
            pltpu.VMEM((16, 256), F32),
        ),
        in_specs=[hbm] * 6,
        out_specs=(vmem,) * 8,
        scratch_shapes=[
            pltpu.VMEM((2, 2, 2, 2, 2, 2, 2, 2, 16, 128), BF16),
            pltpu.VMEM((512, 2048), BF16),
            pltpu.VMEM((2, 512, 256), BF16),
            pltpu.VMEM((TOKEN_BLOCKS, 512, 512 // TOKEN_BLOCKS), BF16),
            pltpu.VMEM((TOKEN_BLOCKS, 512, 512 // TOKEN_BLOCKS), BF16),
            pltpu.VMEM((512, 512), BF16),
            pltpu.VMEM((TOKEN_BLOCKS, 512, 512 // TOKEN_BLOCKS), F32),
            pltpu.VMEM((2, 2, 2, 2, 2, 2, 2, 16, 128), BF16),
            pltpu.VMEM((2, 2, 7, 2, 2, 16, 128), BF16),
            pltpu.VMEM((2, 2, 2, 2, 2, 2, 2, 16, 128), BF16),
            pltpu.VMEM((2, 2, 2, 2, 2, 16, 128), F32),
            pltpu.VMEM((2, 2, 2, 2, 2, 16, 128), F32),
            pltpu.VMEM((7, 2, 2, 16, 128), BF16),
            dma((9 + 2 * len(DEPTHS),)),
            dma((TOKEN_BLOCKS,)),
            dma((TOKEN_BLOCKS,)),
            dma((4, 2, 2)),
            dma((4, 2, 2)),
            dma((2, 2)),
            dma((2, 2)),
        ],
        compiler_params=pltpu.CompilerParams(
            collective_id=0, has_side_effects=True, vmem_limit_bytes=24 * 1024 * 1024
        ),
    )(*(pltpu.with_memory_space_constraint(a, pltpu.HBM) for a in operands))


def expand_kernel(
    own,
    other,
    own_new,
    own_update,
    proj,
    weight,
    first_in,
    second_in,
    new_weight,
    update,
    first_out,
    second_out,
    new_v,
    update_v,
    sems,
    state_sems,
):
    c = lax.axis_index("mp") % 2
    copies = [
        pltpu.make_async_copy(first_in, first_out, state_sems.at[0]),
        pltpu.make_async_copy(second_in, second_out, state_sems.at[1]),
    ]
    for copy in copies:
        copy.start()

    def store(new, upd, core, i, rows, here):
        for n, (src, dst) in enumerate(((new, new_weight), (upd, update))):
            copy = pltpu.make_async_copy(src.at[i], dst.at[rows, here], sems.at[core, n, i])
            copy.start()
            copies.append(copy)

    depth = weight.shape[0]
    for core, normalized in ((0, own), (1, other)):
        for i, (rows, columns, here) in enumerate(column_tiles(depth, c if core == 0 else 1 - c)):
            if core == 0 and i < EARLY_TILES:
                store(own_new, own_update, core, i, rows, here)
                continue
            expanded = jnp.dot(proj[rows, :], normalized[:, columns], preferred_element_type=F32)
            new_v[core, i] = weight[rows, here] - step_rate * expanded
            update_v[core, i] = expanded.astype(BF16)
            store(new_v.at[core], update_v.at[core], core, i, rows, here)
    for copy in copies:
        copy.wait()


def expand(*operands):
    depth = operands[4].shape[0]
    tiles = 2 * depth // ROW_TILE
    vmem = pl.BlockSpec(memory_space=pltpu.VMEM)
    hbm = pl.BlockSpec(memory_space=pltpu.HBM)
    return pl.pallas_call(
        expand_kernel,
        out_shape=(
            jax.ShapeDtypeStruct((depth, 1024), F32),
            jax.ShapeDtypeStruct((depth, 1024), BF16),
            jax.ShapeDtypeStruct((16, 256), F32),
            jax.ShapeDtypeStruct((16, 256), F32),
        ),
        in_specs=[vmem] * 8,
        out_specs=(hbm,) * 4,
        scratch_shapes=[
            pltpu.VMEM((2, tiles, ROW_TILE, 256), F32),
            pltpu.VMEM((2, tiles, ROW_TILE, 256), BF16),
            pltpu.SemaphoreType.DMA((2, 2, tiles)),
            pltpu.SemaphoreType.DMA((2,)),
        ],
        compiler_params=pltpu.CompilerParams(vmem_limit_bytes=20 * 1024 * 1024),
    )(*operands)


def local(activations, out_grads, projector, weight, first_moment, second_moment):
    return tuple(
        expand(*reduce_and_gather(activations, out_grads, projector, weight, first_moment, second_moment))
    )


def solution(mesh):
    in_specs = (
        P("dp", "mp"),
        P("dp", None),
        P("mp", None),
        P("mp", None),
        P("dp", "mp"),
        P("dp", "mp"),
    )
    out_specs = (P("mp", None), P("mp", None), P("dp", "mp"), P("dp", "mp"))
    return jax.shard_map(local, mesh=mesh, in_specs=in_specs, out_specs=out_specs, check_vma=False)
```

```python
import functools

import jax
import jax.numpy as jnp
from jax import lax
from jax.experimental import pallas as pl
from jax.experimental.pallas import tpu as pltpu
from jax.sharding import PartitionSpec as P

first_decay = 0.9
second_decay = 0.999
first_bias = 1.0 - 0.9**2
second_bias = 1.0 - 0.999**2
epsilon = 1e-08
step_rate = 0.00025

MESH = pl.DeviceIdType.MESH
F32 = jnp.float32
BF16 = jnp.bfloat16
TOKEN_BLOCKS = 4
DEPTHS = (768, 512, 512, 256)
EARLY_TILES = 2
ROW_TILE = 512


WRAP_FIRST = ((False, False, True), (True, True, False))
HALVES = (1, 0)
PIECES = ((0, 1), (0, 0), (1, 1), (1, 0))
ARRIVING = ((0, 0), (0, 1), (1, 0), (1, 1))


def place(wrap_first, v):
    return (v // 2, v % 2) if wrap_first else ((v + v // 2) % 2, v // 2)


MASKS = (7, 6, 5, 3, 4, 2, 1)


def bits(m):
    return m // 4, m // 2 % 2, m % 2


def reduce_kernel(
    acts,
    grads,
    proj,
    weight,
    first_moment,
    second_moment,
    own,
    other,
    own_new,
    own_update,
    proj_v,
    weight_v,
    first_new_ref,
    second_new_ref,
    gathered,
    acts_v,
    grads_v,
    mine,
    theirs,
    both,
    summed,
    parts,
    got1,
    sums,
    moments,
    states,
    seven,
    load_sem,
    pair_send,
    pair_recv,
    send_sem,
    recv_sem,
    fw_send,
    fw_recv,
):
    dp = lax.axis_index("dp")
    mp = lax.axis_index("mp")
    zh, c = mp // 2, mp % 2
    chip = (dp // 8, (dp // 2) % 4, zh * 2 + dp % 2)
    sibling = (dp, zh * 2 + 1 - c)

    terms = []
    for axis, v in enumerate(chip):
        options = (v, v + 1 - 2 * (v % 2), 3 - v)
        if axis == 2:
            terms.append([(o % 2, o // 2 * 2 + c) for o in options])
        else:
            terms.append([(o * (8, 2)[axis], 0) for o in options])

    def partner(half, flips, m):
        x, y, z = (
            terms[axis][(2 if WRAP_FIRST[half][axis] == (flips == 1) else 1) if bit else 0]
            for axis, bit in enumerate(bits(m))
        )
        return (x[0] + y[0] + z[0], z[1])

    def flip(at, m):
        return tuple(1 - v if bit else v for v, bit in zip(at, bits(m)))

    sets, members = [], []
    for half in range(2):
        places = [place(w, v) for w, v in zip(WRAP_FIRST[half], chip)]
        sets.append(tuple(p[0] for p in places))
        members.append(tuple(p[1] for p in places))

    load_parts = []

    def depth_part(k):
        return pl.ds(sum(DEPTHS[:k]), DEPTHS[k])

    def load_part(k):
        at = depth_part(k)
        for n, (src, dst) in enumerate(((proj.at[at], proj_v.at[at]), (acts.at[:, at], acts_v.at[:, at]))):
            copy = pltpu.make_async_copy(src, dst, load_sem.at[2 * k + n])
            copy.start()
            load_parts.append(copy)

    load_part(0)
    barrier = pltpu.get_barrier_semaphore()
    for device in [sibling] + [partner(0, flips, m) for flips in (1, 2) for m in MASKS]:
        pl.semaphore_signal(barrier, inc=1, device_id=device, device_id_type=MESH)
    for k in range(1, len(DEPTHS)):
        load_part(k)
    load_grads = []
    for half in range(2):
        for h in range(2):
            columns = pl.ds(pl.multiple_of(h * 512 + c * 256 + half * 128, 128), 128)
            copy = pltpu.make_async_copy(
                grads.at[:, columns],
                grads_v.at[half, :, pl.ds(h * 128, 128)],
                load_sem.at[2 * len(DEPTHS) + 2 * half + h],
            )
            copy.start()
            load_grads.append(copy)
    load_moments = []
    for half in range(2):
        columns = pl.ds(half * 128, 128)
        for n, moment in enumerate((first_moment, second_moment)):
            copy = pltpu.make_async_copy(
                moment.at[:, columns],
                moments.at[(half, *members[half], n)],
                load_sem.at[4 + 2 * len(DEPTHS) + 2 * half + n],
            )
            copy.start()
            load_moments.append(copy)
    load_weight = pltpu.make_async_copy(weight, weight_v, load_sem.at[8 + 2 * len(DEPTHS)])

    started = []

    def send(src, dst, sent, arrived, device):
        copy = pltpu.make_async_remote_copy(
            src_ref=src, dst_ref=dst, send_sem=sent, recv_sem=arrived, device_id=device, device_id_type=MESH
        )
        copy.start()
        started.append(copy)
        return copy

    groups = []

    def spread(stage, piece, half, flips, source, target=None):
        at = (stage, piece, half)
        groups.append(at)
        for n, m in enumerate(MASKS):
            src = source(m)
            dst = src if target is None else target(n)
            pltpu.make_async_remote_copy(
                src_ref=src,
                dst_ref=dst,
                send_sem=send_sem.at[at],
                recv_sem=recv_sem.at[at],
                device_id=partner(half, flips, m),
                device_id_type=MESH,
            ).start()

    def arrived(stage, piece, half):
        pltpu.make_async_copy(seven, seven, recv_sem.at[stage, piece, half]).wait()

    for k in range(len(DEPTHS)):
        at = depth_part(k)
        load_parts[2 * k].wait()
        load_parts[2 * k + 1].wait()
        product = jnp.dot(acts_v[:, at], proj_v[at, :], preferred_element_type=F32)
        projected = product if k == 0 else projected + product
    block = projected.shape[0] // TOKEN_BLOCKS
    pair = []
    for t in range(TOKEN_BLOCKS):
        turned = projected[t * block : (t + 1) * block].T
        summed[t] = turned
        mine[t] = turned.astype(BF16)
        if t == 0:
            pl.semaphore_wait(barrier, 15)
        pair.append(send(mine.at[t], theirs.at[t], pair_send.at[t], pair_recv.at[t], sibling))
    for copy in load_moments:
        copy.wait()
    for half in HALVES:
        spread(0, 0, half, 2, lambda m: moments.at[(half, *members[half])])

    for copy in load_grads:
        copy.wait()
    load_weight.start()
    for t in range(TOKEN_BLOCKS):
        pair[t].wait_recv()
        both[:, t * block : (t + 1) * block] = (summed[t] + theirs[t].astype(F32)).astype(BF16)

    def scatter(piece, half):
        spread(
            1,
            piece,
            half,
            1,
            lambda m: parts.at[(half, *flip(sets[half], m), piece)],
            lambda n: got1.at[half, piece, n],
        )

    for piece, half in PIECES:
        blocks = [x for x in range(4) if place(WRAP_FIRST[half][0], x)[1] == piece]
        left = jnp.concatenate([both[x * 128 : (x + 1) * 128, :] for x in blocks], axis=0)
        product = jnp.dot(left, grads_v[half], preferred_element_type=F32).astype(BF16)
        for i, x in enumerate(blocks):
            for y in range(4):
                for z in range(4):
                    row, column = i * 128 + y * 32 + z % 2 * 16, z // 2 * 128
                    at = [place(w, v) for w, v in zip(WRAP_FIRST[half], (x, y, z))]
                    index = tuple(p[0] for p in at) + tuple(p[1] for p in at)
                    parts[(half, *index)] = product[row : row + 16, column : column + 128]
        scatter(piece, half)

    for piece, half in ARRIVING:
        arrived(1, piece, half)
        total = parts[(half, *sets[half], piece)].astype(F32)
        for n in range(7):
            total += got1[half, piece, n].astype(F32)
        here = (half, *members[half], piece)
        sums[here] = total.astype(BF16)
        spread(2, piece, half, 2, lambda m: sums.at[here])

    for half in HALVES:
        arrived(0, 0, half)
    for piece, half in PIECES:
        arrived(2, piece, half)
        for j in range(2):
            for k in range(2):
                coefficients = sums[half, 0, 0, 0, piece, j, k].astype(F32)
                for n in range(1, 8):
                    coefficients += sums[(half, *bits(n), piece, j, k)].astype(F32)
                first_new = first_decay * moments[half, piece, j, k, 0] + (1.0 - first_decay) * coefficients
                second_new = (
                    second_decay * moments[half, piece, j, k, 1]
                    + (1.0 - second_decay) * coefficients * coefficients
                )
                normalized = first_new / first_bias / (jnp.sqrt(second_new / second_bias) + epsilon)
                gathered[(c, half, *sets[half], piece, j, k)] = normalized.astype(BF16)
                states[half, piece, j, k, 0] = first_new
                states[half, piece, j, k, 1] = second_new
        spread(3, piece, half, 1, lambda m: gathered.at[(c, half, *sets[half], piece)])
    for half in range(2):
        columns = slice(half * 128, (half + 1) * 128)
        first_new_ref[:, columns] = states[(half, *members[half], 0)]
        second_new_ref[:, columns] = states[(half, *members[half], 1)]

    forwards = ([], [])
    for piece, half in ARRIVING:
        arrived(3, piece, half)
        block = gathered.at[c, half, :, :, :, piece]
        forwards[half].append(send(block, block, fw_send.at[piece, half], fw_recv.at[piece, half], sibling))

    def order(core, half, target):
        for x in range(4):
            for y in range(4):
                for z in range(4):
                    row, column = x * 128 + y * 32 + z % 2 * 16, z // 2 * 256 + half * 128
                    at = [place(w, v) for w, v in zip(WRAP_FIRST[half], (x, y, z))]
                    index = tuple(p[0] for p in at) + tuple(p[1] for p in at)
                    target[row : row + 16, column : column + 128] = gathered[(core, half, *index)]

    for half in HALVES:
        order(c, half, own)
    load_weight.wait()
    for i, (rows, columns, here) in enumerate(column_tiles(weight_v.shape[0], c)):
        if i < EARLY_TILES:
            expanded = jnp.dot(proj_v[rows, :], own[:, columns], preferred_element_type=F32)
            own_new[i] = weight_v[rows, here] - step_rate * expanded
            own_update[i] = expanded.astype(BF16)

    for at in groups:
        pltpu.make_async_copy(seven, seven, send_sem.at[at]).wait()
    for copy in started:
        copy.wait_send()
    for half in range(2):
        for copy in forwards[half]:
            copy.wait_recv()
        order(1 - c, half, other)


def column_tiles(depth, core):
    for h in range(2):
        for i in range(depth // ROW_TILE):
            rows = pl.ds(i * ROW_TILE, ROW_TILE)
            yield rows, pl.ds(h * 256, 256), pl.ds(pl.multiple_of(h * 512 + core * 256, 256), 256)


def reduce_and_gather(*operands):
    proj, weight = operands[2], operands[3]
    vmem = pl.BlockSpec(memory_space=pltpu.VMEM)
    hbm = pl.BlockSpec(memory_space=pltpu.HBM)
    dma = pltpu.SemaphoreType.DMA
    return pl.pallas_call(
        reduce_kernel,
        out_shape=(
            pltpu.VMEM((512, 512), BF16),
            pltpu.VMEM((512, 512), BF16),
            pltpu.VMEM((EARLY_TILES, ROW_TILE, 256), F32),
            pltpu.VMEM((EARLY_TILES, ROW_TILE, 256), BF16),
            pltpu.VMEM(proj.shape, BF16),
            pltpu.VMEM(weight.shape, F32),
            pltpu.VMEM((16, 256), F32),
            pltpu.VMEM((16, 256), F32),
        ),
        in_specs=[hbm] * 6,
        out_specs=(vmem,) * 8,
        scratch_shapes=[
            pltpu.VMEM((2, 2, 2, 2, 2, 2, 2, 2, 16, 128), BF16),
            pltpu.VMEM((512, 2048), BF16),
            pltpu.VMEM((2, 512, 256), BF16),
            pltpu.VMEM((TOKEN_BLOCKS, 512, 512 // TOKEN_BLOCKS), BF16),
            pltpu.VMEM((TOKEN_BLOCKS, 512, 512 // TOKEN_BLOCKS), BF16),
            pltpu.VMEM((512, 512), BF16),
            pltpu.VMEM((TOKEN_BLOCKS, 512, 512 // TOKEN_BLOCKS), F32),
            pltpu.VMEM((2, 2, 2, 2, 2, 2, 2, 16, 128), BF16),
            pltpu.VMEM((2, 2, 7, 2, 2, 16, 128), BF16),
            pltpu.VMEM((2, 2, 2, 2, 2, 2, 2, 16, 128), BF16),
            pltpu.VMEM((2, 2, 2, 2, 2, 16, 128), F32),
            pltpu.VMEM((2, 2, 2, 2, 2, 16, 128), F32),
            pltpu.VMEM((7, 2, 2, 16, 128), BF16),
            dma((9 + 2 * len(DEPTHS),)),
            dma((TOKEN_BLOCKS,)),
            dma((TOKEN_BLOCKS,)),
            dma((4, 2, 2)),
            dma((4, 2, 2)),
            dma((2, 2)),
            dma((2, 2)),
        ],
        compiler_params=pltpu.CompilerParams(
            collective_id=0, has_side_effects=True, vmem_limit_bytes=24 * 1024 * 1024
        ),
    )(*(pltpu.with_memory_space_constraint(a, pltpu.HBM) for a in operands))


def expand_kernel(
    own,
    other,
    own_new,
    own_update,
    proj,
    weight,
    first_in,
    second_in,
    new_weight,
    update,
    first_out,
    second_out,
    new_v,
    update_v,
    sems,
    state_sems,
):
    c = lax.axis_index("mp") % 2
    copies = [
        pltpu.make_async_copy(first_in, first_out, state_sems.at[0]),
        pltpu.make_async_copy(second_in, second_out, state_sems.at[1]),
    ]
    for copy in copies:
        copy.start()

    def store(new, upd, core, i, rows, here):
        for n, (src, dst) in enumerate(((new, new_weight), (upd, update))):
            copy = pltpu.make_async_copy(src.at[i], dst.at[rows, here], sems.at[core, n, i])
            copy.start()
            copies.append(copy)

    depth = weight.shape[0]
    for core, normalized in ((0, own), (1, other)):
        for i, (rows, columns, here) in enumerate(column_tiles(depth, c if core == 0 else 1 - c)):
            if core == 0 and i < EARLY_TILES:
                store(own_new, own_update, core, i, rows, here)
                continue
            expanded = jnp.dot(proj[rows, :], normalized[:, columns], preferred_element_type=F32)
            new_v[core, i] = weight[rows, here] - step_rate * expanded
            update_v[core, i] = expanded.astype(BF16)
            store(new_v.at[core], update_v.at[core], core, i, rows, here)
    for copy in copies:
        copy.wait()


def expand(*operands):
    depth = operands[4].shape[0]
    tiles = 2 * depth // ROW_TILE
    vmem = pl.BlockSpec(memory_space=pltpu.VMEM)
    hbm = pl.BlockSpec(memory_space=pltpu.HBM)
    return pl.pallas_call(
        expand_kernel,
        out_shape=(
            jax.ShapeDtypeStruct((depth, 1024), F32),
            jax.ShapeDtypeStruct((depth, 1024), BF16),
            jax.ShapeDtypeStruct((16, 256), F32),
            jax.ShapeDtypeStruct((16, 256), F32),
        ),
        in_specs=[vmem] * 8,
        out_specs=(hbm,) * 4,
        scratch_shapes=[
            pltpu.VMEM((2, tiles, ROW_TILE, 256), F32),
            pltpu.VMEM((2, tiles, ROW_TILE, 256), BF16),
            pltpu.SemaphoreType.DMA((2, 2, tiles)),
            pltpu.SemaphoreType.DMA((2,)),
        ],
        compiler_params=pltpu.CompilerParams(vmem_limit_bytes=20 * 1024 * 1024),
    )(*operands)


def local(activations, out_grads, projector, weight, first_moment, second_moment):
    return tuple(
        expand(*reduce_and_gather(activations, out_grads, projector, weight, first_moment, second_moment))
    )


def solution(mesh):
    in_specs = (
        P("dp", "mp"),
        P("dp", None),
        P("mp", None),
        P("mp", None),
        P("dp", "mp"),
        P("dp", "mp"),
    )
    out_specs = (P("mp", None), P("mp", None), P("dp", "mp"), P("dp", "mp"))
    return jax.shard_map(local, mesh=mesh, in_specs=in_specs, out_specs=out_specs, check_vma=False)
```

```python
import functools

import jax
import jax.numpy as jnp
from jax import lax
from jax.experimental import pallas as pl
from jax.experimental.pallas import tpu as pltpu
from jax.sharding import PartitionSpec as P

first_decay = 0.9
second_decay = 0.999
first_bias = 1.0 - 0.9**2
second_bias = 1.0 - 0.999**2
epsilon = 1e-08
step_rate = 0.00025

MESH = pl.DeviceIdType.MESH
F32 = jnp.float32
BF16 = jnp.bfloat16
TOKEN_BLOCKS = 4
DEPTHS = (768, 512, 512, 256)
EARLY_TILES = 2
ROW_TILE = 512


WRAP_FIRST = ((False, False, True), (True, True, False))
HALVES = (1, 0)
PIECES = ((0, 1), (0, 0), (1, 1), (1, 0))
ARRIVING = ((0, 0), (0, 1), (1, 0), (1, 1))


def place(wrap_first, v):
    return (v // 2, v % 2) if wrap_first else ((v + v // 2) % 2, v // 2)


MASKS = (7, 6, 5, 3, 4, 2, 1)


def bits(m):
    return m // 4, m // 2 % 2, m % 2


def reduce_kernel(
    acts,
    grads,
    proj,
    weight,
    first_moment,
    second_moment,
    own,
    other,
    own_new,
    own_update,
    proj_v,
    weight_v,
    first_new_ref,
    second_new_ref,
    gathered,
    acts_v,
    grads_v,
    mine,
    theirs,
    both,
    summed,
    parts,
    got1,
    sums,
    moments,
    states,
    seven,
    load_sem,
    pair_send,
    pair_recv,
    send_sem,
    recv_sem,
    fw_send,
    fw_recv,
):
    dp = lax.axis_index("dp")
    mp = lax.axis_index("mp")
    zh, c = mp // 2, mp % 2
    chip = (dp // 8, (dp // 2) % 4, zh * 2 + dp % 2)
    sibling = (dp, zh * 2 + 1 - c)

    terms = []
    for axis, v in enumerate(chip):
        options = (v, v + 1 - 2 * (v % 2), 3 - v)
        if axis == 2:
            terms.append([(o % 2, o // 2 * 2 + c) for o in options])
        else:
            terms.append([(o * (8, 2)[axis], 0) for o in options])

    def partner(half, flips, m):
        x, y, z = (
            terms[axis][(2 if WRAP_FIRST[half][axis] == (flips == 1) else 1) if bit else 0]
            for axis, bit in enumerate(bits(m))
        )
        return (x[0] + y[0] + z[0], z[1])

    def flip(at, m):
        return tuple(1 - v if bit else v for v, bit in zip(at, bits(m)))

    sets, members = [], []
    for half in range(2):
        places = [place(w, v) for w, v in zip(WRAP_FIRST[half], chip)]
        sets.append(tuple(p[0] for p in places))
        members.append(tuple(p[1] for p in places))

    load_parts = []

    def depth_part(k):
        return pl.ds(sum(DEPTHS[:k]), DEPTHS[k])

    def load_part(k):
        at = depth_part(k)
        for n, (src, dst) in enumerate(((proj.at[at], proj_v.at[at]), (acts.at[:, at], acts_v.at[:, at]))):
            copy = pltpu.make_async_copy(src, dst, load_sem.at[2 * k + n])
            copy.start()
            load_parts.append(copy)

    load_part(0)
    barrier = pltpu.get_barrier_semaphore()
    for device in [sibling] + [partner(0, flips, m) for flips in (1, 2) for m in MASKS]:
        pl.semaphore_signal(barrier, inc=1, device_id=device, device_id_type=MESH)
    for k in range(1, len(DEPTHS)):
        load_part(k)
    load_grads = []
    for half in range(2):
        for h in range(2):
            columns = pl.ds(pl.multiple_of(h * 512 + c * 256 + half * 128, 128), 128)
            copy = pltpu.make_async_copy(
                grads.at[:, columns],
                grads_v.at[half, :, pl.ds(h * 128, 128)],
                load_sem.at[2 * len(DEPTHS) + 2 * half + h],
            )
            copy.start()
            load_grads.append(copy)
    load_moments = []
    for half in range(2):
        columns = pl.ds(half * 128, 128)
        for n, moment in enumerate((first_moment, second_moment)):
            copy = pltpu.make_async_copy(
                moment.at[:, columns],
                moments.at[(half, *members[half], n)],
                load_sem.at[4 + 2 * len(DEPTHS) + 2 * half + n],
            )
            copy.start()
            load_moments.append(copy)
    load_weight = pltpu.make_async_copy(weight, weight_v, load_sem.at[8 + 2 * len(DEPTHS)])

    started = []

    def send(src, dst, sent, arrived, device):
        copy = pltpu.make_async_remote_copy(
            src_ref=src, dst_ref=dst, send_sem=sent, recv_sem=arrived, device_id=device, device_id_type=MESH
        )
        copy.start()
        started.append(copy)
        return copy

    groups = []

    def spread(stage, piece, half, flips, source, target=None):
        at = (stage, piece, half)
        groups.append(at)
        for n, m in enumerate(MASKS):
            src = source(m)
            dst = src if target is None else target(n)
            pltpu.make_async_remote_copy(
                src_ref=src,
                dst_ref=dst,
                send_sem=send_sem.at[at],
                recv_sem=recv_sem.at[at],
                device_id=partner(half, flips, m),
                device_id_type=MESH,
            ).start()

    def arrived(stage, piece, half):
        pltpu.make_async_copy(seven, seven, recv_sem.at[stage, piece, half]).wait()

    for k in range(len(DEPTHS)):
        at = depth_part(k)
        load_parts[2 * k].wait()
        load_parts[2 * k + 1].wait()
        product = jnp.dot(acts_v[:, at], proj_v[at, :], preferred_element_type=F32)
        projected = product if k == 0 else projected + product
    block = projected.shape[0] // TOKEN_BLOCKS
    pair = []
    for t in range(TOKEN_BLOCKS):
        turned = projected[t * block : (t + 1) * block].T
        summed[t] = turned
        mine[t] = turned.astype(BF16)
        if t == 0:
            pl.semaphore_wait(barrier, 15)
        pair.append(send(mine.at[t], theirs.at[t], pair_send.at[t], pair_recv.at[t], sibling))
    for copy in load_moments:
        copy.wait()
    for half in HALVES:
        spread(0, 0, half, 2, lambda m: moments.at[(half, *members[half])])

    for copy in load_grads:
        copy.wait()
    for t in range(TOKEN_BLOCKS):
        pair[t].wait_recv()
        both[:, t * block : (t + 1) * block] = (summed[t] + theirs[t].astype(F32)).astype(BF16)

    def scatter(piece, half):
        spread(
            1,
            piece,
            half,
            1,
            lambda m: parts.at[(half, *flip(sets[half], m), piece)],
            lambda n: got1.at[half, piece, n],
        )

    for piece, half in PIECES:
        blocks = [x for x in range(4) if place(WRAP_FIRST[half][0], x)[1] == piece]
        left = jnp.concatenate([both[x * 128 : (x + 1) * 128, :] for x in blocks], axis=0)
        product = jnp.dot(left, grads_v[half], preferred_element_type=F32).astype(BF16)
        for i, x in enumerate(blocks):
            for y in range(4):
                for z in range(4):
                    row, column = i * 128 + y * 32 + z % 2 * 16, z // 2 * 128
                    at = [place(w, v) for w, v in zip(WRAP_FIRST[half], (x, y, z))]
                    index = tuple(p[0] for p in at) + tuple(p[1] for p in at)
                    parts[(half, *index)] = product[row : row + 16, column : column + 128]
        scatter(piece, half)
    load_weight.start()

    for piece, half in ARRIVING:
        arrived(1, piece, half)
        total = parts[(half, *sets[half], piece)].astype(F32)
        for n in range(7):
            total += got1[half, piece, n].astype(F32)
        here = (half, *members[half], piece)
        sums[here] = total.astype(BF16)
        spread(2, piece, half, 2, lambda m: sums.at[here])

    for half in HALVES:
        arrived(0, 0, half)
    for piece, half in PIECES:
        arrived(2, piece, half)
        for j in range(2):
            for k in range(2):
                coefficients = sums[half, 0, 0, 0, piece, j, k].astype(F32)
                for n in range(1, 8):
                    coefficients += sums[(half, *bits(n), piece, j, k)].astype(F32)
                first_new = first_decay * moments[half, piece, j, k, 0] + (1.0 - first_decay) * coefficients
                second_new = (
                    second_decay * moments[half, piece, j, k, 1]
                    + (1.0 - second_decay) * coefficients * coefficients
                )
                normalized = first_new / first_bias / (jnp.sqrt(second_new / second_bias) + epsilon)
                gathered[(c, half, *sets[half], piece, j, k)] = normalized.astype(BF16)
                states[half, piece, j, k, 0] = first_new
                states[half, piece, j, k, 1] = second_new
        spread(3, piece, half, 1, lambda m: gathered.at[(c, half, *sets[half], piece)])
    for half in range(2):
        columns = slice(half * 128, (half + 1) * 128)
        first_new_ref[:, columns] = states[(half, *members[half], 0)]
        second_new_ref[:, columns] = states[(half, *members[half], 1)]

    forwards = ([], [])
    for piece, half in ARRIVING:
        arrived(3, piece, half)
        block = gathered.at[c, half, :, :, :, piece]
        forwards[half].append(send(block, block, fw_send.at[piece, half], fw_recv.at[piece, half], sibling))

    def order(core, half, target):
        for x in range(4):
            for y in range(4):
                for z in range(4):
                    row, column = x * 128 + y * 32 + z % 2 * 16, z // 2 * 256 + half * 128
                    at = [place(w, v) for w, v in zip(WRAP_FIRST[half], (x, y, z))]
                    index = tuple(p[0] for p in at) + tuple(p[1] for p in at)
                    target[row : row + 16, column : column + 128] = gathered[(core, half, *index)]

    for half in HALVES:
        order(c, half, own)
    load_weight.wait()
    for i, (rows, columns, here) in enumerate(column_tiles(weight_v.shape[0], c)):
        if i < EARLY_TILES:
            expanded = jnp.dot(proj_v[rows, :], own[:, columns], preferred_element_type=F32)
            own_new[i] = weight_v[rows, here] - step_rate * expanded
            own_update[i] = expanded.astype(BF16)

    for at in groups:
        pltpu.make_async_copy(seven, seven, send_sem.at[at]).wait()
    for copy in started:
        copy.wait_send()
    for half in range(2):
        for copy in forwards[half]:
            copy.wait_recv()
        order(1 - c, half, other)


def column_tiles(depth, core):
    for h in range(2):
        for i in range(depth // ROW_TILE):
            rows = pl.ds(i * ROW_TILE, ROW_TILE)
            yield rows, pl.ds(h * 256, 256), pl.ds(pl.multiple_of(h * 512 + core * 256, 256), 256)


def reduce_and_gather(*operands):
    proj, weight = operands[2], operands[3]
    vmem = pl.BlockSpec(memory_space=pltpu.VMEM)
    hbm = pl.BlockSpec(memory_space=pltpu.HBM)
    dma = pltpu.SemaphoreType.DMA
    return pl.pallas_call(
        reduce_kernel,
        out_shape=(
            pltpu.VMEM((512, 512), BF16),
            pltpu.VMEM((512, 512), BF16),
            pltpu.VMEM((EARLY_TILES, ROW_TILE, 256), F32),
            pltpu.VMEM((EARLY_TILES, ROW_TILE, 256), BF16),
            pltpu.VMEM(proj.shape, BF16),
            pltpu.VMEM(weight.shape, F32),
            pltpu.VMEM((16, 256), F32),
            pltpu.VMEM((16, 256), F32),
        ),
        in_specs=[hbm] * 6,
        out_specs=(vmem,) * 8,
        scratch_shapes=[
            pltpu.VMEM((2, 2, 2, 2, 2, 2, 2, 2, 16, 128), BF16),
            pltpu.VMEM((512, 2048), BF16),
            pltpu.VMEM((2, 512, 256), BF16),
            pltpu.VMEM((TOKEN_BLOCKS, 512, 512 // TOKEN_BLOCKS), BF16),
            pltpu.VMEM((TOKEN_BLOCKS, 512, 512 // TOKEN_BLOCKS), BF16),
            pltpu.VMEM((512, 512), BF16),
            pltpu.VMEM((TOKEN_BLOCKS, 512, 512 // TOKEN_BLOCKS), F32),
            pltpu.VMEM((2, 2, 2, 2, 2, 2, 2, 16, 128), BF16),
            pltpu.VMEM((2, 2, 7, 2, 2, 16, 128), BF16),
            pltpu.VMEM((2, 2, 2, 2, 2, 2, 2, 16, 128), BF16),
            pltpu.VMEM((2, 2, 2, 2, 2, 16, 128), F32),
            pltpu.VMEM((2, 2, 2, 2, 2, 16, 128), F32),
            pltpu.VMEM((7, 2, 2, 16, 128), BF16),
            dma((9 + 2 * len(DEPTHS),)),
            dma((TOKEN_BLOCKS,)),
            dma((TOKEN_BLOCKS,)),
            dma((4, 2, 2)),
            dma((4, 2, 2)),
            dma((2, 2)),
            dma((2, 2)),
        ],
        compiler_params=pltpu.CompilerParams(
            collective_id=0, has_side_effects=True, vmem_limit_bytes=24 * 1024 * 1024
        ),
    )(*(pltpu.with_memory_space_constraint(a, pltpu.HBM) for a in operands))


def expand_kernel(
    own,
    other,
    own_new,
    own_update,
    proj,
    weight,
    first_in,
    second_in,
    new_weight,
    update,
    first_out,
    second_out,
    new_v,
    update_v,
    sems,
    state_sems,
):
    c = lax.axis_index("mp") % 2
    copies = [
        pltpu.make_async_copy(first_in, first_out, state_sems.at[0]),
        pltpu.make_async_copy(second_in, second_out, state_sems.at[1]),
    ]
    for copy in copies:
        copy.start()

    def store(new, upd, core, i, rows, here):
        for n, (src, dst) in enumerate(((new, new_weight), (upd, update))):
            copy = pltpu.make_async_copy(src.at[i], dst.at[rows, here], sems.at[core, n, i])
            copy.start()
            copies.append(copy)

    depth = weight.shape[0]
    for core, normalized in ((0, own), (1, other)):
        for i, (rows, columns, here) in enumerate(column_tiles(depth, c if core == 0 else 1 - c)):
            if core == 0 and i < EARLY_TILES:
                store(own_new, own_update, core, i, rows, here)
                continue
            expanded = jnp.dot(proj[rows, :], normalized[:, columns], preferred_element_type=F32)
            new_v[core, i] = weight[rows, here] - step_rate * expanded
            update_v[core, i] = expanded.astype(BF16)
            store(new_v.at[core], update_v.at[core], core, i, rows, here)
    for copy in copies:
        copy.wait()


def expand(*operands):
    depth = operands[4].shape[0]
    tiles = 2 * depth // ROW_TILE
    vmem = pl.BlockSpec(memory_space=pltpu.VMEM)
    hbm = pl.BlockSpec(memory_space=pltpu.HBM)
    return pl.pallas_call(
        expand_kernel,
        out_shape=(
            jax.ShapeDtypeStruct((depth, 1024), F32),
            jax.ShapeDtypeStruct((depth, 1024), BF16),
            jax.ShapeDtypeStruct((16, 256), F32),
            jax.ShapeDtypeStruct((16, 256), F32),
        ),
        in_specs=[vmem] * 8,
        out_specs=(hbm,) * 4,
        scratch_shapes=[
            pltpu.VMEM((2, tiles, ROW_TILE, 256), F32),
            pltpu.VMEM((2, tiles, ROW_TILE, 256), BF16),
            pltpu.SemaphoreType.DMA((2, 2, tiles)),
            pltpu.SemaphoreType.DMA((2,)),
        ],
        compiler_params=pltpu.CompilerParams(vmem_limit_bytes=20 * 1024 * 1024),
    )(*operands)


def local(activations, out_grads, projector, weight, first_moment, second_moment):
    return tuple(
        expand(*reduce_and_gather(activations, out_grads, projector, weight, first_moment, second_moment))
    )


def solution(mesh):
    in_specs = (
        P("dp", "mp"),
        P("dp", None),
        P("mp", None),
        P("mp", None),
        P("dp", "mp"),
        P("dp", "mp"),
    )
    out_specs = (P("mp", None), P("mp", None), P("dp", "mp"), P("dp", "mp"))
    return jax.shard_map(local, mesh=mesh, in_specs=in_specs, out_specs=out_specs, check_vma=False)
```
